256 devices in a mesh: pair: 4 (over z_hi), row: 8 (over z_lo, y), col: 8 (over x, core).
Axes of the slice: x: 4, y: 4, z: 8 (z_hi: 4, z_lo: 2; z = z_hi * 2 + z_lo), core: 2. Of those that a mesh axis runs over, the one named last changes fastest.
Arguments:
- conductance: float32 [2048, 4096], P('row', 'col'), may hold values from 0.25 to 4
- valid_mask: int32 [2048, 4096], P('row', 'col'), may hold values 0 or 1
- focal_cells: int32 [8, 2], P('pair'), may hold values from 0 to 8388607
- initial_volts: float32 [8, 2048, 4096], P('pair', 'row', 'col'), may hold values from -2 to 2
Outputs:
- voltages: float32 [8, 2048, 4096], P('pair', 'row', 'col')
- current_sum: float32 [2048, 4096], P('row', 'col')
- current_max: float32 [2048, 4096], P('row', 'col')
The draws below stay inside these ranges and needn't reach their ends.
All inputs are finite; a program needn't handle non-finite values. No bound on the sum of `valid_mask` on one device may be relied on, other than what follows from the above.
Results may differ from the reference program's by a relative error of at most 0.0039.
Values sent between devices are 32-bit elements; how exact they have to be, the bound alone decides.
A program may use at most 64 MiB of HBM per device.

```python
import math
import jax
import jax.numpy as jnp
from jax import lax

ITERS = 6
NX = 2048
NY = 4096
PAIRS = 8


def wave_field(key, low_amp, high_amp):
    row_frac = (jnp.arange(NX, dtype=jnp.float32) / NX)[None, :, None]
    col_frac = (jnp.arange(NY, dtype=jnp.float32) / NY)[None, None, :]
    smooth = jnp.zeros((PAIRS, NX, NY), jnp.float32)
    for wave_index in range(3):
        wave_key = jax.random.fold_in(key, wave_index)
        subkeys = jax.random.split(wave_key, 4)
        wave_rows = jax.random.randint(subkeys[0], (PAIRS, 1, 1), 1, 4).astype(jnp.float32)
        wave_cols = jax.random.randint(subkeys[1], (PAIRS, 1, 1), 1, 4).astype(jnp.float32)
        phases = jax.random.uniform(subkeys[2], (PAIRS, 1, 1), jnp.float32, -math.pi, math.pi)
        amplitude = jax.random.uniform(subkeys[3], (PAIRS, 1, 1), jnp.float32, low_amp, high_amp)
        smooth = smooth + amplitude * jnp.cos(2.0 * math.pi * (wave_rows * row_frac + wave_cols * col_frac) + phases)
    return smooth


def draw_initial_volts(key, part):
    key = jax.random.fold_in(key, 7)
    wave_key, noise_key = jax.random.split(key)
    smooth = wave_field(wave_key, 0.2, 0.4)
    noise_part = 0.01 * jnp.clip(jax.random.normal(noise_key, (PAIRS, NX, NY), jnp.float32), -4.0, 4.0)
    return smooth + noise_part


def place_ends(array, stream_key, least, high):
    extent = array.shape
    place = [jax.random.randint(jax.random.fold_in(stream_key, axis), (), 0, extent[axis]) for axis in range(len(extent))]
    array = array.at[tuple(place)].set(least)
    longest = extent.index(max(extent))
    place[longest] = (place[longest] + 1) % extent[longest]
    return array.at[tuple(place)].set(high)


def block_levels(stream_key, extent, cuts, smallest, high):
    loudness, own = 1.0, jax.random.fold_in(stream_key, 6)
    for axis_at, shards_of in cuts:
        steps = jnp.exp(jax.random.uniform(jax.random.fold_in(own, axis_at), (shards_of,), jnp.float32, smallest / len(cuts), high / len(cuts)))
        loudness = loudness * jnp.repeat(steps, extent[axis_at] // shards_of).reshape([-1 if axis == axis_at else 1 for axis in range(len(extent))])
    return loudness


def setup_inputs(seed: int = 0) -> dict:
    splits = jax.random.split(jax.random.key(seed), 5)
    return {
        "conductance": jnp.clip(jnp.exp(math.log(4.0) - 2.7725887 * jax.random.uniform(splits[0], (NX, NY), jnp.float32) ** block_levels(splits[0], (NX, NY), ((0, 8), (1, 8)), -0.2, 0.2)), 0.25, 4.0),
        "valid_mask": place_ends((jax.random.randint(splits[1], (NX, NY), 0, 16) < 15).astype(jnp.int32), jax.random.fold_in(splits[1], 1), 0, 1),
        "focal_cells": place_ends(jax.random.randint(splits[2], (PAIRS, 2), 0, NX * NY), jax.random.fold_in(splits[2], 1), 0, (NX * NY) - 1).astype(jnp.int32),
        "initial_volts": draw_initial_volts(jax.random.fold_in(splits[4], 71), 0),
    }


LEAKAGE = 0.01


def link_set(padded_cond, padded_valid):
    centre_cond = padded_cond[1:-1, 1:-1]
    centre_valid = padded_valid[1:-1, 1:-1]

    def link_value(other_cond, other_valid):
        return 0.5 * (centre_cond + other_cond) * centre_valid * other_valid

    north = link_value(padded_cond[:-2, 1:-1], padded_valid[:-2, 1:-1])
    south = link_value(padded_cond[2:, 1:-1], padded_valid[2:, 1:-1])
    west = link_value(padded_cond[1:-1, :-2], padded_valid[1:-1, :-2])
    east = link_value(padded_cond[1:-1, 2:], padded_valid[1:-1, 2:])
    diagonal = north + south + west + east + LEAKAGE * centre_cond + (1.0 - centre_valid)
    inverse = 1.0 / jnp.maximum(diagonal, 1.0)
    return (north, south, west, east, diagonal), inverse


def apply_padded(field, wide, links):
    north, south, west, east, diagonal = links
    beside = north * wide[..., :-2, 1:-1] + south * wide[..., 2:, 1:-1]
    beside = beside + west * wide[..., 1:-1, :-2] + east * wide[..., 1:-1, 2:]
    return diagonal * field - beside


def cell_current(field, wide, links):
    north, south, west, east, diagonal = links
    flows = jnp.abs(north * (field - wide[..., :-2, 1:-1])) + jnp.abs(south * (field - wide[..., 2:, 1:-1]))
    flows = flows + jnp.abs(west * (field - wide[..., 1:-1, :-2])) + jnp.abs(east * (field - wide[..., 1:-1, 2:]))
    return 0.5 * flows


def reference(conductance, valid_mask, focal_cells, initial_volts):
    valid = valid_mask.astype(jnp.float32)
    cond = conductance * valid
    links, inverse = link_set(jnp.pad(cond, 1), jnp.pad(valid, 1))
    flat_index = jnp.arange(NX * NY, dtype=jnp.int32).reshape(NX, NY)

    def operate(field):
        return apply_padded(field, jnp.pad(field, 1), links)

    def solve_one(inputs):
        start, cells = inputs
        inject = (flat_index == cells[0]).astype(jnp.float32) - (flat_index == cells[1]).astype(jnp.float32)
        voltage = start
        residual = inject - operate(voltage)
        scaled = inverse * residual
        search = scaled
        progress = jnp.sum(residual * scaled)
        for iteration in range(ITERS):
            image = operate(search)
            step_size = progress / jnp.sum(search * image)
            voltage = voltage + step_size * search
            residual = residual - step_size * image
            scaled = inverse * residual
            renewed = jnp.sum(residual * scaled)
            search = scaled + (renewed / progress) * search
            progress = renewed
        current = cell_current(voltage, jnp.pad(voltage, 1), links)
        return voltage, current

    voltages, currents = lax.map(solve_one, (initial_volts, focal_cells))
    return voltages, jnp.sum(currents, axis=0), jnp.max(currents, axis=0)
```

```python
import functools

import jax
import jax.numpy as jnp
from jax import lax
from jax.experimental import pallas as pl
from jax.experimental.pallas import tpu as pltpu
from jax.sharding import PartitionSpec as P

MESH = pl.DeviceIdType.MESH
LEAKAGE = 0.01
STEPS = 6
LANES = 128
EDGE = 8
OWN = 16
HIGH = jax.lax.Precision.HIGHEST


def lane_ids():
    return lax.broadcasted_iota(jnp.int32, (8, LANES), 1)


def east(tiles):
    last = lane_ids() == LANES - 1
    rolled = [pltpu.roll(tile, LANES - 1, 1) for tile in tiles]
    return [jnp.where(last, rolled[(t + 1) % len(tiles)], rolled[t]) for t in range(len(tiles))]


def west(tiles):
    first = lane_ids() == 0
    rolled = [pltpu.roll(tile, 1, 1) for tile in tiles]
    return [jnp.where(first, rolled[t - 1], rolled[t]) for t in range(len(tiles))]


def link(a, b):
    return jnp.where(jnp.minimum(a, b) > 0.0, 0.5 * (a + b), 0.0)


def solve_coefficients(totals):
    same = [totals[2 * k] for k in range(STEPS)]
    after = [totals[2 * k + 1] for k in range(STEPS)]
    nu = [same[1], after[1]]
    for k in range(1, STEPS - 1):
        nu.append(2.0 * same[k + 1] - nu[0])
        nu.append(2.0 * after[k + 1] - nu[1])
    rho = [same[0], after[0], nu[0]]
    for k in range(1, STEPS - 2):
        rho.append(2.0 * nu[k] - rho[k])
    gram = [[None] * STEPS for _ in range(STEPS)]
    gram[0][0] = rho[0] - rho[1]
    for j in range(1, STEPS):
        gram[0][j] = rho[j] - nu[j - 1]
    for i in range(STEPS - 1):
        for j in range(i, STEPS - 1):
            before = abs(j - 1)
            gram[i + 1][j + 1] = 0.5 * (nu[i + j] + nu[abs(i - j)]) - 0.25 * (
                nu[i + j + 1] + nu[abs(i - j - 1)] + nu[i + before] + nu[abs(i - before)]
            )
    right = list(rho)
    least = [3e-7 * gram[j][j] for j in range(STEPS)]
    inverse, factors = [], {}
    for j in range(STEPS):
        pivot = gram[j][j]
        usable = pivot > least[j]
        inverse.append(jnp.where(usable, 1.0 / jnp.where(usable, pivot, 1.0), 0.0))
        for i in range(j + 1, STEPS):
            factors[i, j] = gram[j][i] * inverse[j]
        for i in range(j + 1, STEPS):
            for m in range(i, STEPS):
                gram[i][m] = gram[i][m] - factors[i, j] * gram[j][m]
            right[i] = right[i] - factors[i, j] * right[j]
    out = [right[j] * inverse[j] for j in range(STEPS)]
    for i in reversed(range(STEPS)):
        for j in range(i + 1, STEPS):
            out[i] = out[i] - factors[j, i] * out[j]
    return out


def kernel(
    sizes,
    cond_in,
    mask_in,
    focal,
    volts_in,
    volts_out,
    sum_out,
    max_out,
    stage_cond,
    stage_mask,
    volts,
    cond,
    link_e,
    link_n,
    scale,
    coef_c,
    coef_e,
    coef_n,
    basis,
    pack_e,
    pack_w,
    land_w,
    land_e,
    dots,
    message,
    gather_col,
    gather_row,
    local,
    far,
    from_prev,
    from_next,
    result,
    load_sem,
    store_sem,
    halo_send,
    halo_recv,
    red_send,
    red_recv,
    ring_send,
    ring_recv,
):
    pairs, rows, tiles, n_pair, n_row, n_col = sizes
    wide = tiles + 1
    chunks = rows // 8
    fold = rows // 4
    fold_chunks = fold // 8
    quarter = rows // 4
    unit = quarter // 4
    my_pair, my_row, my_col = lax.axis_index("pair"), lax.axis_index("row"), lax.axis_index("col")

    def around(index, step, count):
        return lax.rem(index + (step + count), count)

    loads = []
    for t in range(tiles):
        lanes = pl.ds(t * LANES, LANES)
        loads.append(pltpu.make_async_copy(cond_in.at[:, lanes], stage_cond.at[t], load_sem.at[len(loads)]))
        loads.append(pltpu.make_async_copy(mask_in.at[:, lanes], stage_mask.at[t], load_sem.at[len(loads)]))
        for p in range(pairs):
            loads.append(
                pltpu.make_async_copy(
                    volts_in.at[p, :, lanes], volts.at[p, t, pl.ds(OWN, rows)], load_sem.at[len(loads)]
                )
            )
    for load in loads:
        load.start()

    north, south = around(my_row, -1, n_row), around(my_row, 1, n_row)
    westward, eastward = around(my_col, -1, n_col), around(my_col, 1, n_col)
    before, after = around(my_pair, -1, n_pair), around(my_pair, 1, n_pair)
    partners = [{"col": around(my_col, step, n_col)} for step in range(1, n_col)]
    partners += [{"row": around(my_row, step, n_row)} for step in range(1, n_row)]
    partners += [{"row": r, "col": c} for r in (north, south) for c in (westward, eastward)]
    partners += [{"pair": before}, {"pair": after}]
    barrier = pltpu.get_barrier_semaphore()
    for partner in partners:
        pl.semaphore_signal(barrier, inc=1, device_id=partner, device_id_type=MESH)

    zero = jnp.zeros((8, LANES), jnp.float32)
    for start in (0, rows + 3 * 8):
        at = pl.ds(start, 8)
        for t in range(wide):
            for ref in (cond, scale, link_n, coef_n):
                ref[t, at, :] = zero
            for p in range(pairs):
                volts[p, t, at, :] = zero
                for k in range(STEPS):
                    basis[k, p, t, at, :] = zero

    for load in loads:
        load.wait()

    def own_cond(c, carry):
        at = pl.ds(pl.multiple_of(8 * c, 8), 8)
        to = pl.ds(pl.multiple_of(OWN + 8 * c, 8), 8)
        for t in range(tiles):
            cond[t, to, :] = stage_cond[t, at, :] * stage_mask[t, at, :].astype(jnp.float32)
        return carry

    lax.fori_loop(0, chunks, own_cond, 0)

    lane = lane_ids()

    def pack(c, carry):
        for side, tile, ref in ((0, 0, pack_w), (1, tiles - 1, pack_e)):
            packed = jnp.zeros((8, LANES), jnp.float32)
            for g in range(4):
                at = pl.ds(pl.multiple_of(OWN + g * fold + 8 * c, 8), 8)
                fields = [volts[p, tile, at, :] for p in range(pairs)] + [cond[tile, at, :]]
                for f, value in enumerate(fields):
                    low = 32 * g + 8 * f
                    first = 0 if side == 0 else LANES - 8
                    shift = (low - first) % LANES
                    moved = pltpu.roll(value, shift, 1) if shift else value
                    packed = jnp.where((lane >= low) & (lane < low + 8), moved, packed)
            ref[pl.ds(pl.multiple_of(8 * c, 8), 8), :] = packed
        return carry

    lax.fori_loop(0, fold_chunks, pack, 0)
    pl.semaphore_wait(barrier, len(partners))

    top, bottom = pl.ds(OWN, 8), pl.ds(OWN + rows - 8, 8)
    over, under = pl.ds(OWN - 8, 8), pl.ds(OWN + rows, 8)
    mid = pl.ds(8, fold)
    halo = [
        (volts.at[:, pl.ds(0, tiles), top], volts.at[:, pl.ds(0, tiles), under], {"row": north}),
        (cond.at[pl.ds(0, tiles), top], cond.at[pl.ds(0, tiles), under], {"row": north}),
        (volts.at[:, pl.ds(0, tiles), bottom], volts.at[:, pl.ds(0, tiles), over], {"row": south}),
        (cond.at[pl.ds(0, tiles), bottom], cond.at[pl.ds(0, tiles), over], {"row": south}),
        (pack_w, land_e.at[mid], {"col": westward}),
        (pack_e, land_w.at[mid], {"col": eastward}),
        (pack_w.at[pl.ds(0, 8)], land_e.at[pl.ds(fold + 8, 8)], {"row": north, "col": westward}),
        (pack_w.at[pl.ds(fold - 8, 8)], land_e.at[pl.ds(0, 8)], {"row": south, "col": westward}),
        (pack_e.at[pl.ds(0, 8)], land_w.at[pl.ds(fold + 8, 8)], {"row": north, "col": eastward}),
        (pack_e.at[pl.ds(fold - 8, 8)], land_w.at[pl.ds(0, 8)], {"row": south, "col": eastward}),
    ]
    halo = [
        pltpu.make_async_remote_copy(
            src_ref=src,
            dst_ref=dst,
            send_sem=halo_send.at[i],
            recv_sem=halo_recv.at[i],
            device_id=who,
            device_id_type=MESH,
        )
        for i, (src, dst, who) in enumerate(halo)
    ]
    for copy in halo:
        copy.start()
    for copy in halo:
        copy.wait()

    has_n = (my_row > 0).astype(jnp.float32)
    has_s = (my_row < n_row - 1).astype(jnp.float32)
    has_w = (my_col > 0).astype(jnp.float32)
    has_e = (my_col < n_col - 1).astype(jnp.float32)
    for t in range(tiles):
        cond[t, over, :] = cond[t, over, :] * has_n
        cond[t, under, :] = cond[t, under, :] * has_s

    def unpack(source, g, to, keep):
        left = land_w[source, :]
        right = land_e[source, :]
        for f in range(pairs + 1):
            low = 32 * g + 8 * f
            a = pltpu.roll(left, (LANES - 8 - low) % LANES, 1)
            b = pltpu.roll(right, (LANES - low) % LANES, 1) if low else right
            if f == pairs:
                a, b = a * (has_w * keep), b * (has_e * keep)
            value = jnp.where(lane < 8, b, jnp.where(lane >= LANES - 8, a, 0.0))
            if f == pairs:
                cond[tiles, to, :] = value
            else:
                volts[f, tiles, to, :] = value

    def unpack_chunk(c, carry):
        for g in range(4):
            unpack(
                pl.ds(pl.multiple_of(8 + 8 * c, 8), 8),
                g,
                pl.ds(pl.multiple_of(OWN + g * fold + 8 * c, 8), 8),
                1.0,
            )
        return carry

    lax.fori_loop(0, fold_chunks, unpack_chunk, 0)
    unpack(pl.ds(0, 8), 3, over, has_n)
    unpack(pl.ds(fold + 8, 8), 0, under, has_s)

    def links_chunk(c, carry):
        start = pl.multiple_of(8 + 8 * c, 8)
        at = pl.ds(start, 8)
        here = [cond[t, at, :] for t in range(wide)]
        right = [link(a, b) for a, b in zip(here, east(here))]
        left = west(right)
        for t in range(wide):
            up = link(here[t], cond[t, pl.ds(start - 1, 8), :])
            down = link(here[t], cond[t, pl.ds(start + 1, 8), :])
            diagonal = up + down + left[t] + right[t] + LEAKAGE * here[t] + jnp.where(here[t] > 0.0, 0.0, 1.0)
            most = jnp.maximum(diagonal, 1.0)
            root = lax.rsqrt(most)
            root = root * (1.5 - 0.5 * most * root * root)
            link_e[t, at, :] = right[t]
            link_n[t, at, :] = up
            scale[t, at, :] = root
            coef_c[t, at, :] = 2.0 * jnp.maximum(1.0 - diagonal, 0.0)
        return carry

    lax.fori_loop(0, chunks + 2, links_chunk, 0)

    width_all = tiles * LANES * n_col
    sub = lax.broadcasted_iota(jnp.int32, (8, LANES), 0)
    columns = [my_col * (tiles * LANES) + t * LANES + lane for t in range(tiles)]
    columns.append(my_col * (tiles * LANES) + jnp.where(lane < 64, tiles * LANES, -LANES) + lane)

    def start_chunk(c, carry):
        start = pl.multiple_of(8 + 8 * c, 8)
        at, up_at, down_at = pl.ds(start, 8), pl.ds(start - 1, 8), pl.ds(start + 1, 8)
        root = [scale[t, at, :] for t in range(wide)]
        right = [link_e[t, at, :] for t in range(wide)]
        up = [link_n[t, at, :] for t in range(wide)]
        root_e = east(root)
        flat = (my_row * rows + 8 * c - 8 + sub) * width_all
        own = []
        for t in range(wide):
            coef_e[t, at, :] = 2.0 * right[t] * root[t] * root_e[t]
            coef_n[t, at, :] = 2.0 * up[t] * root[t] * scale[t, up_at, :]
            value = cond[t, at, :]
            own.append(LEAKAGE * value + jnp.where(value > 0.0, 0.0, 1.0))
        for p in range(pairs):
            here = [volts[p, t, at, :] for t in range(wide)]
            there = east(here)
            flow = [right[t] * (here[t] - there[t]) for t in range(wide)]
            flow_w = west(flow)
            for t in range(wide):
                total = flow[t] - flow_w[t] + own[t] * here[t]
                total = total + up[t] * (here[t] - volts[p, t, up_at, :])
                total = total + link_n[t, down_at, :] * (here[t] - volts[p, t, down_at, :])
                cell = flat + columns[t]
                inject = jnp.where(cell == focal[p, 0], 1.0, 0.0) - jnp.where(cell == focal[p, 1], 1.0, 0.0)
                basis[0, p, t, at, :] = root[t] * (inject - total)
        return carry

    lax.fori_loop(0, chunks + 2, start_chunk, 0)

    def advance(k, c, sums):
        start = pl.multiple_of(8 + 8 * c, 8)
        at, up_at, down_at = pl.ds(start, 8), pl.ds(start - 1, 8), pl.ds(start + 1, 8)
        final = k == STEPS - 1
        count = tiles if final else wide
        right = [coef_e[t, at, :] for t in range(wide)]
        out = []
        for p in range(pairs):
            here = [basis[k, p, t, at, :] for t in range(wide)]
            there = east(here)
            back = west([right[t] * here[t] for t in range(wide)])
            same = jnp.zeros((8, LANES), jnp.float32)
            step = jnp.zeros((8, LANES), jnp.float32)
            for t in range(count):
                value = coef_c[t, at, :] * here[t] + right[t] * there[t] + back[t]
                value = value + coef_n[t, at, :] * basis[k, p, t, up_at, :]
                value = value + coef_n[t, down_at, :] * basis[k, p, t, down_at, :]
                value = 0.5 * value if k < 2 else value - basis[k - 1, p, t, at, :]
                if not final:
                    basis[k + 1, p, t, at, :] = value
                if sums is not None and t < tiles:
                    same = same + here[t] * here[t]
                    step = step + here[t] * value
            if sums is not None:
                out += [sums[2 * p] + same, sums[2 * p + 1] + step]
        return tuple(out)

    for k in range(STEPS):
        if k < STEPS - 1:

            def border(i, carry, k=k):
                advance(k, i * (chunks + 1), None)
                return carry

            lax.fori_loop(0, 2, border, 0)
        sums = lax.fori_loop(1, chunks + 1, functools.partial(advance, k), (zero,) * (2 * pairs))
        for p in range(pairs):
            dots[(2 * k) * pairs + p] = sums[2 * p]
            dots[(2 * k + 1) * pairs + p] = sums[2 * p + 1]

    n_dots = 2 * STEPS * pairs
    part = jnp.sum(dots[...], axis=1)
    message[...] = jnp.broadcast_to(jnp.sum(part, axis=1, keepdims=True), (n_dots, LANES))

    def reduce_over(axis, me, count, source, gather, phase):
        copies = []
        for step in range(1, count):
            copies.append(
                pltpu.make_async_remote_copy(
                    src_ref=source,
                    dst_ref=gather.at[me],
                    send_sem=red_send.at[phase, step - 1],
                    recv_sem=red_recv.at[phase, step - 1],
                    device_id={axis: around(me, step, count)},
                    device_id_type=MESH,
                )
            )
        for copy in copies:
            copy.start()
        gather[me] = source[...]
        for copy in copies:
            copy.wait()
        total = gather[0]
        for i in range(1, count):
            total = total + gather[i]
        return total

    message[...] = reduce_over("col", my_col, n_col, message, gather_col, 0)
    totals = reduce_over("row", my_row, n_row, message, gather_row, 1)
    parts = solve_coefficients([totals[j * pairs : (j + 1) * pairs] for j in range(2 * STEPS)])
    weights = [[jnp.broadcast_to(part[p : p + 1], (8, LANES)) for part in parts] for p in range(pairs)]

    def volts_chunk(c, carry):
        at = pl.ds(pl.multiple_of(8 + 8 * c, 8), 8)
        for t in range(wide):
            root = scale[t, at, :]
            for p in range(pairs):
                change = weights[p][0] * basis[0, p, t, at, :]
                for k in range(1, STEPS):
                    change = change + weights[p][k] * basis[k, p, t, at, :]
                volts[p, t, at, :] = volts[p, t, at, :] + root * change
        return carry

    lax.fori_loop(0, chunks + 2, volts_chunk, 0)
    stores = []
    for t in range(tiles):
        for p in range(pairs):
            stores.append(
                pltpu.make_async_copy(
                    volts.at[p, t, pl.ds(OWN, rows)],
                    volts_out.at[p, :, pl.ds(t * LANES, LANES)],
                    store_sem.at[len(stores)],
                )
            )
    for store in stores:
        store.start()

    def currents(index):
        def body(i, carry):
            row = index * quarter + 8 * i
            start = pl.multiple_of(OWN + row, 8)
            at, up_at, down_at = pl.ds(start, 8), pl.ds(start - 1, 8), pl.ds(start + 1, 8)
            right = [link_e[t, at, :] for t in range(wide)]
            total, peak = [None] * tiles, [None] * tiles
            for p in range(pairs):
                here = [volts[p, t, at, :] for t in range(wide)]
                there = east(here)
                flow = [jnp.abs(right[t] * (here[t] - there[t])) for t in range(wide)]
                flow_w = west(flow)
                for t in range(tiles):
                    value = flow[t] + flow_w[t]
                    value = value + jnp.abs(link_n[t, at, :] * (here[t] - volts[p, t, up_at, :]))
                    value = value + jnp.abs(link_n[t, down_at, :] * (here[t] - volts[p, t, down_at, :]))
                    value = 0.5 * value
                    total[t] = value if p == 0 else total[t] + value
                    peak[t] = value if p == 0 else jnp.maximum(peak[t], value)
            to = pl.ds(pl.multiple_of(row, 8), 8)
            for t in range(tiles):
                local[0, to, pl.ds(t * LANES, LANES)] = total[t]
                local[1, to, pl.ds(t * LANES, LANES)] = peak[t]
            return carry

        lax.fori_loop(0, quarter // 8, body, 0)

    q_next, q_prev = around(my_pair, 1, n_pair), around(my_pair, -1, n_pair)
    q_far = around(my_pair, 2, n_pair)

    def span(index, u):
        return pl.ds(pl.multiple_of(index * quarter + u * unit, unit), unit)

    def ring(slot, src, dst, who):
        copy = pltpu.make_async_remote_copy(
            src_ref=src,
            dst_ref=dst,
            send_sem=ring_send.at[slot],
            recv_sem=ring_recv.at[slot],
            device_id={"pair": who},
            device_id_type=MESH,
        )
        copy.start()
        return copy

    in_unit = [pl.ds(u * unit, unit) for u in range(4)]
    sent = {}
    currents(q_far)
    for i in range(2):
        sent["far", i] = ring(i, local.at[:, span(q_far, i)], far.at[:, in_unit[i]], q_next)
        sent["far", 2 + i] = ring(2 + i, local.at[:, span(q_far, 2 + i)], far.at[:, in_unit[2 + i]], q_prev)
    currents(q_next)
    for u in (2, 3):
        sent["prev", u] = ring(4 + u, local.at[:, span(q_next, u)], from_prev.at[:, in_unit[u]], q_next)
    currents(q_prev)
    for u in (0, 1):
        sent["next", u] = ring(8 + u, local.at[:, span(q_prev, u)], from_next.at[:, in_unit[u]], q_prev)
    currents(my_pair)
    for i in range(2):
        for u, owner, name, base, target in (
            (i, q_next, "prev", 4, from_prev),
            (2 + i, q_prev, "next", 8, from_next),
        ):
            sent["far", u].wait_recv()
            at = span(owner, u)
            local[0, at, :] = local[0, at, :] + far[0, in_unit[u], :]
            local[1, at, :] = jnp.maximum(local[1, at, :], far[1, in_unit[u], :])
            sent[name, u] = ring(base + u, local.at[:, at], target.at[:, in_unit[u]], owner)
    for u in (0, 2, 1, 3):
        sent["prev", u].wait_recv()
        sent["next", u].wait_recv()
        at = span(my_pair, u)
        result[0, at, :] = local[0, at, :] + from_prev[0, in_unit[u], :] + from_next[0, in_unit[u], :]
        result[1, at, :] = jnp.maximum(
            local[1, at, :], jnp.maximum(from_prev[1, in_unit[u], :], from_next[1, in_unit[u], :])
        )
        sent["up", u] = ring(12 + u, result.at[:, at], result.at[:, at], q_next)
        sent["down", u] = ring(16 + u, result.at[:, at], result.at[:, at], q_prev)
    for i in range(2):
        sent["up", i].wait_recv()
        at = span(q_prev, i)
        sent["over", i] = ring(20 + i, result.at[:, at], result.at[:, at], q_next)
        sent["down", 2 + i].wait_recv()
        at = span(q_next, 2 + i)
        sent["over", 2 + i] = ring(22 + i, result.at[:, at], result.at[:, at], q_prev)
    for i in range(2):
        sent["up", 2 + i].wait_recv()
        sent["down", i].wait_recv()

    def keep(index, number):
        at = pl.ds(pl.multiple_of(index * quarter, quarter), quarter)
        base = pairs * tiles + 2 * number
        for i, ref in enumerate((sum_out, max_out)):
            stores.append(pltpu.make_async_copy(result.at[i, at], ref.at[at], store_sem.at[base + i]))
            stores[-1].start()

    keep(my_pair, 0)
    keep(q_prev, 1)
    keep(q_next, 2)
    for u in range(4):
        sent["over", u].wait_recv()
    keep(q_far, 3)
    for copy in sent.values():
        copy.wait_send()
    for store in stores:
        store.wait()


def on_device(mesh_sizes, conductance, valid_mask, focal_cells, initial_volts):
    rows, columns = conductance.shape
    pairs = initial_volts.shape[0]
    tiles = columns // LANES
    n_pair, n_row, n_col = mesh_sizes
    sizes = (pairs, rows, tiles, n_pair, n_row, n_col)
    wide, tall, fold, quarter = tiles + 1, rows + 32, rows // 4, rows // 4
    n_dots = 2 * STEPS * pairs
    f32 = jnp.float32
    anywhere = pl.BlockSpec(memory_space=pl.ANY)
    field = pltpu.VMEM((wide, tall, LANES), f32)
    return pl.pallas_call(
        functools.partial(kernel, sizes),
        out_shape=(
            jax.ShapeDtypeStruct((pairs, rows, columns), f32),
            jax.ShapeDtypeStruct((rows, columns), f32),
            jax.ShapeDtypeStruct((rows, columns), f32),
        ),
        in_specs=[anywhere, anywhere, pl.BlockSpec(memory_space=pltpu.SMEM), anywhere],
        out_specs=(anywhere, anywhere, anywhere),
        scratch_shapes=[
            pltpu.VMEM((tiles, rows, LANES), f32),
            pltpu.VMEM((tiles, rows, LANES), jnp.int32),
            pltpu.VMEM((pairs, wide, tall, LANES), f32),
            field,
            field,
            field,
            field,
            field,
            field,
            field,
            pltpu.VMEM((STEPS, pairs, wide, tall, LANES), f32),
            pltpu.VMEM((fold, LANES), f32),
            pltpu.VMEM((fold, LANES), f32),
            pltpu.VMEM((fold + 16, LANES), f32),
            pltpu.VMEM((fold + 16, LANES), f32),
            pltpu.VMEM((n_dots, 8, LANES), f32),
            pltpu.VMEM((n_dots, LANES), f32),
            pltpu.VMEM((n_col, n_dots, LANES), f32),
            pltpu.VMEM((n_row, n_dots, LANES), f32),
            pltpu.VMEM((2, rows, columns), f32),
            pltpu.VMEM((2, quarter, columns), f32),
            pltpu.VMEM((2, quarter, columns), f32),
            pltpu.VMEM((2, quarter, columns), f32),
            pltpu.VMEM((2, rows, columns), f32),
            pltpu.SemaphoreType.DMA(((2 + pairs) * tiles,)),
            pltpu.SemaphoreType.DMA((pairs * tiles + 8,)),
            pltpu.SemaphoreType.DMA((10,)),
            pltpu.SemaphoreType.DMA((10,)),
            pltpu.SemaphoreType.DMA((2, max(n_col, n_row) - 1)),
            pltpu.SemaphoreType.DMA((2, max(n_col, n_row) - 1)),
            pltpu.SemaphoreType.DMA((24,)),
            pltpu.SemaphoreType.DMA((24,)),
        ],
        compiler_params=pltpu.CompilerParams(
            collective_id=0, has_side_effects=True, vmem_limit_bytes=48 * 1024 * 1024
        ),
    )(conductance, valid_mask, focal_cells, initial_volts)


def solution(mesh):
    in_specs = (P("row", "col"), P("row", "col"), P("pair", None), P("pair", "row", "col"))
    out_specs = (P("pair", "row", "col"), P("row", "col"), P("row", "col"))
    sizes = (mesh.shape["pair"], mesh.shape["row"], mesh.shape["col"])
    return jax.shard_map(
        functools.partial(on_device, sizes), mesh=mesh, in_specs=in_specs, out_specs=out_specs, check_vma=False
    )
```

```python
import functools

import jax
import jax.numpy as jnp
from jax import lax
from jax.experimental import pallas as pl
from jax.experimental.pallas import tpu as pltpu
from jax.sharding import PartitionSpec as P

MESH = pl.DeviceIdType.MESH
LEAKAGE = 0.01
STEPS = 6
LANES = 128
EDGE = 8
OWN = 16
BLOCK = 32


def lane_ids(height):
    return lax.broadcasted_iota(jnp.int32, (height, LANES), 1)


def east(tiles):
    last = lane_ids(tiles[0].shape[0]) == LANES - 1
    rolled = [pltpu.roll(tile, LANES - 1, 1) for tile in tiles]
    return [jnp.where(last, rolled[(t + 1) % len(tiles)], rolled[t]) for t in range(len(tiles))]


def west(tiles):
    first = lane_ids(tiles[0].shape[0]) == 0
    rolled = [pltpu.roll(tile, 1, 1) for tile in tiles]
    return [jnp.where(first, rolled[t - 1], rolled[t]) for t in range(len(tiles))]


def link(a, b):
    return jnp.where(jnp.minimum(a, b) > 0.0, 0.5 * (a + b), 0.0)


def solve_coefficients(totals):
    same = [totals[2 * k] for k in range(STEPS)]
    after = [totals[2 * k + 1] for k in range(STEPS)]
    nu = [same[1], after[1]]
    for k in range(1, STEPS - 1):
        nu.append(2.0 * same[k + 1] - nu[0])
        nu.append(2.0 * after[k + 1] - nu[1])
    rho = [same[0], after[0], nu[0]]
    for k in range(1, STEPS - 2):
        rho.append(2.0 * nu[k] - rho[k])
    gram = [[None] * STEPS for _ in range(STEPS)]
    gram[0][0] = rho[0] - rho[1]
    for j in range(1, STEPS):
        gram[0][j] = rho[j] - nu[j - 1]
    for i in range(STEPS - 1):
        for j in range(i, STEPS - 1):
            before = abs(j - 1)
            gram[i + 1][j + 1] = 0.5 * (nu[i + j] + nu[abs(i - j)]) - 0.25 * (
                nu[i + j + 1] + nu[abs(i - j - 1)] + nu[i + before] + nu[abs(i - before)]
            )
    right = list(rho)
    least = [3e-7 * gram[j][j] for j in range(STEPS)]
    inverse, factors = [], {}
    for j in range(STEPS):
        pivot = gram[j][j]
        usable = pivot > least[j]
        inverse.append(jnp.where(usable, 1.0 / jnp.where(usable, pivot, 1.0), 0.0))
        for i in range(j + 1, STEPS):
            factors[i, j] = gram[j][i] * inverse[j]
        for i in range(j + 1, STEPS):
            for m in range(i, STEPS):
                gram[i][m] = gram[i][m] - factors[i, j] * gram[j][m]
            right[i] = right[i] - factors[i, j] * right[j]
    out = [right[j] * inverse[j] for j in range(STEPS)]
    for i in reversed(range(STEPS)):
        for j in range(i + 1, STEPS):
            out[i] = out[i] - factors[j, i] * out[j]
    return out


def kernel(
    sizes,
    cond_in,
    mask_in,
    focal,
    volts_in,
    volts_out,
    sum_out,
    max_out,
    stage_cond,
    stage_mask,
    volts,
    cond,
    link_e,
    link_n,
    scale,
    coef_c,
    coef_e,
    coef_n,
    basis,
    pack_e,
    pack_w,
    land_w,
    land_e,
    dots,
    message,
    gather_col,
    gather_row,
    local,
    far,
    from_prev,
    from_next,
    result,
    load_sem,
    store_sem,
    halo_send,
    halo_recv,
    red_send,
    red_recv,
    ring_send,
    ring_recv,
):
    pairs, rows, tiles, n_pair, n_row, n_col = sizes
    wide = tiles + 1
    chunks = rows // 8
    fold = rows // 4
    fold_chunks = fold // 8
    quarter = rows // 4
    unit = quarter // 4
    my_pair, my_row, my_col = lax.axis_index("pair"), lax.axis_index("row"), lax.axis_index("col")

    def around(index, step, count):
        return lax.rem(index + (step + count), count)

    loads = []
    for t in range(tiles):
        lanes = pl.ds(t * LANES, LANES)
        loads.append(pltpu.make_async_copy(cond_in.at[:, lanes], stage_cond.at[t], load_sem.at[len(loads)]))
        loads.append(pltpu.make_async_copy(mask_in.at[:, lanes], stage_mask.at[t], load_sem.at[len(loads)]))
        for p in range(pairs):
            loads.append(
                pltpu.make_async_copy(
                    volts_in.at[p, :, lanes], volts.at[p, t, pl.ds(OWN, rows)], load_sem.at[len(loads)]
                )
            )
    for load in loads:
        load.start()

    north, south = around(my_row, -1, n_row), around(my_row, 1, n_row)
    westward, eastward = around(my_col, -1, n_col), around(my_col, 1, n_col)
    before, after = around(my_pair, -1, n_pair), around(my_pair, 1, n_pair)
    partners = [{"col": around(my_col, step, n_col)} for step in range(1, n_col)]
    partners += [{"row": around(my_row, step, n_row)} for step in range(1, n_row)]
    partners += [{"row": r, "col": c} for r in (north, south) for c in (westward, eastward)]
    partners += [{"pair": before}, {"pair": after}]
    barrier = pltpu.get_barrier_semaphore()
    for partner in partners:
        pl.semaphore_signal(barrier, inc=1, device_id=partner, device_id_type=MESH)

    zero = jnp.zeros((8, LANES), jnp.float32)
    for start in (0, rows + 3 * 8):
        at = pl.ds(start, 8)
        for t in range(wide):
            for ref in (cond, scale, link_n, coef_n):
                ref[t, at, :] = zero
            for p in range(pairs):
                volts[p, t, at, :] = zero
                for k in range(STEPS):
                    basis[k, p, t, at, :] = zero

    for load in loads:
        load.wait()

    def own_cond(c, carry):
        at = pl.ds(pl.multiple_of(8 * c, 8), 8)
        to = pl.ds(pl.multiple_of(OWN + 8 * c, 8), 8)
        for t in range(tiles):
            cond[t, to, :] = stage_cond[t, at, :] * stage_mask[t, at, :].astype(jnp.float32)
        return carry

    lax.fori_loop(0, chunks, own_cond, 0)

    lane = lane_ids(8)

    def pack(c, carry):
        for side, tile, ref in ((0, 0, pack_w), (1, tiles - 1, pack_e)):
            packed = jnp.zeros((8, LANES), jnp.float32)
            for g in range(4):
                at = pl.ds(pl.multiple_of(OWN + g * fold + 8 * c, 8), 8)
                fields = [volts[p, tile, at, :] for p in range(pairs)] + [cond[tile, at, :]]
                for f, value in enumerate(fields):
                    low = 32 * g + 8 * f
                    first = 0 if side == 0 else LANES - 8
                    shift = (low - first) % LANES
                    moved = pltpu.roll(value, shift, 1) if shift else value
                    packed = jnp.where((lane >= low) & (lane < low + 8), moved, packed)
            ref[pl.ds(pl.multiple_of(8 * c, 8), 8), :] = packed
        return carry

    lax.fori_loop(0, fold_chunks, pack, 0)
    pl.semaphore_wait(barrier, len(partners))

    top, bottom = pl.ds(OWN, 8), pl.ds(OWN + rows - 8, 8)
    over, under = pl.ds(OWN - 8, 8), pl.ds(OWN + rows, 8)
    mid = pl.ds(8, fold)
    halo = [
        (volts.at[:, pl.ds(0, tiles), top], volts.at[:, pl.ds(0, tiles), under], {"row": north}),
        (cond.at[pl.ds(0, tiles), top], cond.at[pl.ds(0, tiles), under], {"row": north}),
        (volts.at[:, pl.ds(0, tiles), bottom], volts.at[:, pl.ds(0, tiles), over], {"row": south}),
        (cond.at[pl.ds(0, tiles), bottom], cond.at[pl.ds(0, tiles), over], {"row": south}),
        (pack_w, land_e.at[mid], {"col": westward}),
        (pack_e, land_w.at[mid], {"col": eastward}),
        (pack_w.at[pl.ds(0, 8)], land_e.at[pl.ds(fold + 8, 8)], {"row": north, "col": westward}),
        (pack_w.at[pl.ds(fold - 8, 8)], land_e.at[pl.ds(0, 8)], {"row": south, "col": westward}),
        (pack_e.at[pl.ds(0, 8)], land_w.at[pl.ds(fold + 8, 8)], {"row": north, "col": eastward}),
        (pack_e.at[pl.ds(fold - 8, 8)], land_w.at[pl.ds(0, 8)], {"row": south, "col": eastward}),
    ]
    halo = [
        pltpu.make_async_remote_copy(
            src_ref=src,
            dst_ref=dst,
            send_sem=halo_send.at[i],
            recv_sem=halo_recv.at[i],
            device_id=who,
            device_id_type=MESH,
        )
        for i, (src, dst, who) in enumerate(halo)
    ]
    for copy in halo:
        copy.start()
    for copy in halo:
        copy.wait()

    has_n = (my_row > 0).astype(jnp.float32)
    has_s = (my_row < n_row - 1).astype(jnp.float32)
    has_w = (my_col > 0).astype(jnp.float32)
    has_e = (my_col < n_col - 1).astype(jnp.float32)
    for t in range(tiles):
        cond[t, over, :] = cond[t, over, :] * has_n
        cond[t, under, :] = cond[t, under, :] * has_s

    def unpack(source, g, to, keep):
        left = land_w[source, :]
        right = land_e[source, :]
        for f in range(pairs + 1):
            low = 32 * g + 8 * f
            a = pltpu.roll(left, (LANES - 8 - low) % LANES, 1)
            b = pltpu.roll(right, (LANES - low) % LANES, 1) if low else right
            if f == pairs:
                a, b = a * (has_w * keep), b * (has_e * keep)
            value = jnp.where(lane < 8, b, jnp.where(lane >= LANES - 8, a, 0.0))
            if f == pairs:
                cond[tiles, to, :] = value
            else:
                volts[f, tiles, to, :] = value

    def unpack_chunk(c, carry):
        for g in range(4):
            unpack(
                pl.ds(pl.multiple_of(8 + 8 * c, 8), 8),
                g,
                pl.ds(pl.multiple_of(OWN + g * fold + 8 * c, 8), 8),
                1.0,
            )
        return carry

    lax.fori_loop(0, fold_chunks, unpack_chunk, 0)
    unpack(pl.ds(0, 8), 3, over, has_n)
    unpack(pl.ds(fold + 8, 8), 0, under, has_s)

    def sweep_own(body, carry=()):
        def step(c, carry):
            return body(pl.multiple_of(OWN + BLOCK * c, 8), BLOCK, carry)

        return lax.fori_loop(0, rows // BLOCK, step, carry)

    def sweep_border(body):
        def step(i, carry):
            return body(pl.multiple_of(OWN - 8 + i * (rows + 8), 8), 8, carry)

        lax.fori_loop(0, 2, step, ())

    def links_rows(start, height, carry):
        at = pl.ds(start, height)
        here = [cond[t, at, :] for t in range(wide)]
        right = [link(a, b) for a, b in zip(here, east(here))]
        left = west(right)
        for t in range(wide):
            up = link(here[t], cond[t, pl.ds(start - 1, height), :])
            down = link(here[t], cond[t, pl.ds(start + 1, height), :])
            diagonal = up + down + left[t] + right[t] + LEAKAGE * here[t] + jnp.where(here[t] > 0.0, 0.0, 1.0)
            most = jnp.maximum(diagonal, 1.0)
            root = lax.rsqrt(most)
            root = root * (1.5 - 0.5 * most * root * root)
            link_e[t, at, :] = right[t]
            link_n[t, at, :] = up
            scale[t, at, :] = root
            coef_c[t, at, :] = 2.0 * jnp.maximum(1.0 - diagonal, 0.0)
        return carry

    sweep_border(links_rows)
    sweep_own(links_rows)

    width_all = tiles * LANES * n_col

    def start_rows(start, height, carry):
        at, up_at, down_at = pl.ds(start, height), pl.ds(start - 1, height), pl.ds(start + 1, height)
        column = lane_ids(height)
        sub = lax.broadcasted_iota(jnp.int32, (height, LANES), 0)
        first = my_col * (tiles * LANES)
        columns = [first + t * LANES + column for t in range(tiles)]
        columns.append(first + jnp.where(column < 64, tiles * LANES, -LANES) + column)
        root = [scale[t, at, :] for t in range(wide)]
        right = [link_e[t, at, :] for t in range(wide)]
        up = [link_n[t, at, :] for t in range(wide)]
        root_e = east(root)
        flat = (my_row * rows + start - OWN + sub) * width_all
        own = []
        for t in range(wide):
            coef_e[t, at, :] = 2.0 * right[t] * root[t] * root_e[t]
            coef_n[t, at, :] = 2.0 * up[t] * root[t] * scale[t, up_at, :]
            value = cond[t, at, :]
            own.append(LEAKAGE * value + jnp.where(value > 0.0, 0.0, 1.0))
        for p in range(pairs):
            here = [volts[p, t, at, :] for t in range(wide)]
            there = east(here)
            flow = [right[t] * (here[t] - there[t]) for t in range(wide)]
            flow_w = west(flow)
            for t in range(wide):
                total = flow[t] - flow_w[t] + own[t] * here[t]
                total = total + up[t] * (here[t] - volts[p, t, up_at, :])
                total = total + link_n[t, down_at, :] * (here[t] - volts[p, t, down_at, :])
                cell = flat + columns[t]
                inject = jnp.where(cell == focal[p, 0], 1.0, 0.0) - jnp.where(cell == focal[p, 1], 1.0, 0.0)
                basis[0, p, t, at, :] = root[t] * (inject - total)
        return carry

    sweep_border(start_rows)
    sweep_own(start_rows)

    def advance(k, start, height, sums):
        at, up_at, down_at = pl.ds(start, height), pl.ds(start - 1, height), pl.ds(start + 1, height)
        final = k == STEPS - 1
        count = tiles if final else wide
        right = [coef_e[t, at, :] for t in range(wide)]
        out = []
        for p in range(pairs):
            here = [basis[k, p, t, at, :] for t in range(wide)]
            there = east(here)
            back = west([right[t] * here[t] for t in range(wide)])
            same = jnp.zeros((height, LANES), jnp.float32)
            step = jnp.zeros((height, LANES), jnp.float32)
            for t in range(count):
                value = coef_c[t, at, :] * here[t] + right[t] * there[t] + back[t]
                value = value + coef_n[t, at, :] * basis[k, p, t, up_at, :]
                value = value + coef_n[t, down_at, :] * basis[k, p, t, down_at, :]
                value = 0.5 * value if k < 2 else value - basis[k - 1, p, t, at, :]
                if not final:
                    basis[k + 1, p, t, at, :] = value
                if sums and t < tiles:
                    same = same + here[t] * here[t]
                    step = step + here[t] * value
            if sums:
                out += [sums[2 * p] + same, sums[2 * p + 1] + step]
        return tuple(out) if sums else sums

    def fold_rows(value):
        total = value[:8]
        for i in range(1, BLOCK // 8):
            total = total + value[8 * i : 8 * i + 8]
        return total

    for k in range(STEPS):
        if k < STEPS - 1:
            sweep_border(functools.partial(advance, k))
        tall_zero = jnp.zeros((BLOCK, LANES), jnp.float32)
        sums = sweep_own(functools.partial(advance, k), (tall_zero,) * (2 * pairs))
        for p in range(pairs):
            dots[(2 * k) * pairs + p] = fold_rows(sums[2 * p])
            dots[(2 * k + 1) * pairs + p] = fold_rows(sums[2 * p + 1])

    n_dots = 2 * STEPS * pairs
    part = jnp.sum(dots[...], axis=1)
    message[...] = jnp.broadcast_to(jnp.sum(part, axis=1, keepdims=True), (n_dots, LANES))

    def reduce_over(axis, me, count, source, gather, phase):
        copies = []
        for step in range(1, count):
            copies.append(
                pltpu.make_async_remote_copy(
                    src_ref=source,
                    dst_ref=gather.at[me],
                    send_sem=red_send.at[phase, step - 1],
                    recv_sem=red_recv.at[phase, step - 1],
                    device_id={axis: around(me, step, count)},
                    device_id_type=MESH,
                )
            )
        for copy in copies:
            copy.start()
        gather[me] = source[...]
        for copy in copies:
            copy.wait()
        total = gather[0]
        for i in range(1, count):
            total = total + gather[i]
        return total

    message[...] = reduce_over("col", my_col, n_col, message, gather_col, 0)
    totals = reduce_over("row", my_row, n_row, message, gather_row, 1)
    parts = solve_coefficients([totals[j * pairs : (j + 1) * pairs] for j in range(2 * STEPS)])
    weights = [[jnp.broadcast_to(part[p : p + 1], (BLOCK, LANES)) for part in parts] for p in range(pairs)]

    def volts_rows(start, height, carry):
        at = pl.ds(start, height)
        for t in range(wide):
            root = scale[t, at, :]
            for p in range(pairs):
                change = weights[p][0][:height] * basis[0, p, t, at, :]
                for k in range(1, STEPS):
                    change = change + weights[p][k][:height] * basis[k, p, t, at, :]
                volts[p, t, at, :] = volts[p, t, at, :] + root * change
        return carry

    sweep_border(volts_rows)
    sweep_own(volts_rows)
    stores = []
    for t in range(tiles):
        for p in range(pairs):
            stores.append(
                pltpu.make_async_copy(
                    volts.at[p, t, pl.ds(OWN, rows)],
                    volts_out.at[p, :, pl.ds(t * LANES, LANES)],
                    store_sem.at[len(stores)],
                )
            )
    for store in stores:
        store.start()

    def currents(index):
        def body(i, carry):
            row = index * quarter + BLOCK * i
            start = pl.multiple_of(OWN + row, 8)
            at, up_at, down_at = pl.ds(start, BLOCK), pl.ds(start - 1, BLOCK), pl.ds(start + 1, BLOCK)
            right = [link_e[t, at, :] for t in range(wide)]
            total, peak = [None] * tiles, [None] * tiles
            for p in range(pairs):
                here = [volts[p, t, at, :] for t in range(wide)]
                there = east(here)
                flow = [jnp.abs(right[t] * (here[t] - there[t])) for t in range(wide)]
                flow_w = west(flow)
                for t in range(tiles):
                    value = flow[t] + flow_w[t]
                    value = value + jnp.abs(link_n[t, at, :] * (here[t] - volts[p, t, up_at, :]))
                    value = value + jnp.abs(link_n[t, down_at, :] * (here[t] - volts[p, t, down_at, :]))
                    value = 0.5 * value
                    total[t] = value if p == 0 else total[t] + value
                    peak[t] = value if p == 0 else jnp.maximum(peak[t], value)
            to = pl.ds(pl.multiple_of(row, 8), BLOCK)
            for t in range(tiles):
                local[0, to, pl.ds(t * LANES, LANES)] = total[t]
                local[1, to, pl.ds(t * LANES, LANES)] = peak[t]
            return carry

        lax.fori_loop(0, quarter // BLOCK, body, 0)

    q_next, q_prev = around(my_pair, 1, n_pair), around(my_pair, -1, n_pair)
    q_far = around(my_pair, 2, n_pair)

    def span(index, u):
        return pl.ds(pl.multiple_of(index * quarter + u * unit, unit), unit)

    def ring(slot, src, dst, who):
        copy = pltpu.make_async_remote_copy(
            src_ref=src,
            dst_ref=dst,
            send_sem=ring_send.at[slot],
            recv_sem=ring_recv.at[slot],
            device_id={"pair": who},
            device_id_type=MESH,
        )
        copy.start()
        return copy

    in_unit = [pl.ds(u * unit, unit) for u in range(4)]
    sent = {}
    currents(q_far)
    for i in range(2):
        sent["far", i] = ring(i, local.at[:, span(q_far, i)], far.at[:, in_unit[i]], q_next)
        sent["far", 2 + i] = ring(2 + i, local.at[:, span(q_far, 2 + i)], far.at[:, in_unit[2 + i]], q_prev)
    currents(q_next)
    for u in (2, 3):
        sent["prev", u] = ring(4 + u, local.at[:, span(q_next, u)], from_prev.at[:, in_unit[u]], q_next)
    currents(q_prev)
    for u in (0, 1):
        sent["next", u] = ring(8 + u, local.at[:, span(q_prev, u)], from_next.at[:, in_unit[u]], q_prev)
    currents(my_pair)
    for i in range(2):
        for u, owner, name, base, target in (
            (i, q_next, "prev", 4, from_prev),
            (2 + i, q_prev, "next", 8, from_next),
        ):
            sent["far", u].wait_recv()
            at = span(owner, u)
            local[0, at, :] = local[0, at, :] + far[0, in_unit[u], :]
            local[1, at, :] = jnp.maximum(local[1, at, :], far[1, in_unit[u], :])
            sent[name, u] = ring(base + u, local.at[:, at], target.at[:, in_unit[u]], owner)
    for u in (0, 2, 1, 3):
        sent["prev", u].wait_recv()
        sent["next", u].wait_recv()
        at = span(my_pair, u)
        result[0, at, :] = local[0, at, :] + from_prev[0, in_unit[u], :] + from_next[0, in_unit[u], :]
        result[1, at, :] = jnp.maximum(
            local[1, at, :], jnp.maximum(from_prev[1, in_unit[u], :], from_next[1, in_unit[u], :])
        )
        sent["up", u] = ring(12 + u, result.at[:, at], result.at[:, at], q_next)
        sent["down", u] = ring(16 + u, result.at[:, at], result.at[:, at], q_prev)
    for i in range(2):
        sent["up", i].wait_recv()
        at = span(q_prev, i)
        sent["over", i] = ring(20 + i, result.at[:, at], result.at[:, at], q_next)
        sent["down", 2 + i].wait_recv()
        at = span(q_next, 2 + i)
        sent["over", 2 + i] = ring(22 + i, result.at[:, at], result.at[:, at], q_prev)
    for i in range(2):
        sent["up", 2 + i].wait_recv()
        sent["down", i].wait_recv()

    def keep(index, number):
        at = pl.ds(pl.multiple_of(index * quarter, quarter), quarter)
        base = pairs * tiles + 2 * number
        for i, ref in enumerate((sum_out, max_out)):
            stores.append(pltpu.make_async_copy(result.at[i, at], ref.at[at], store_sem.at[base + i]))
            stores[-1].start()

    keep(my_pair, 0)
    keep(q_prev, 1)
    keep(q_next, 2)
    for u in range(4):
        sent["over", u].wait_recv()
    keep(q_far, 3)
    for copy in sent.values():
        copy.wait_send()
    for store in stores:
        store.wait()


def on_device(mesh_sizes, conductance, valid_mask, focal_cells, initial_volts):
    rows, columns = conductance.shape
    pairs = initial_volts.shape[0]
    tiles = columns // LANES
    n_pair, n_row, n_col = mesh_sizes
    sizes = (pairs, rows, tiles, n_pair, n_row, n_col)
    wide, tall, fold, quarter = tiles + 1, rows + 32, rows // 4, rows // 4
    n_dots = 2 * STEPS * pairs
    f32 = jnp.float32
    anywhere = pl.BlockSpec(memory_space=pl.ANY)
    field = pltpu.VMEM((wide, tall, LANES), f32)
    return pl.pallas_call(
        functools.partial(kernel, sizes),
        out_shape=(
            jax.ShapeDtypeStruct((pairs, rows, columns), f32),
            jax.ShapeDtypeStruct((rows, columns), f32),
            jax.ShapeDtypeStruct((rows, columns), f32),
        ),
        in_specs=[anywhere, anywhere, pl.BlockSpec(memory_space=pltpu.SMEM), anywhere],
        out_specs=(anywhere, anywhere, anywhere),
        scratch_shapes=[
            pltpu.VMEM((tiles, rows, LANES), f32),
            pltpu.VMEM((tiles, rows, LANES), jnp.int32),
            pltpu.VMEM((pairs, wide, tall, LANES), f32),
            field,
            field,
            field,
            field,
            field,
            field,
            field,
            pltpu.VMEM((STEPS, pairs, wide, tall, LANES), f32),
            pltpu.VMEM((fold, LANES), f32),
            pltpu.VMEM((fold, LANES), f32),
            pltpu.VMEM((fold + 16, LANES), f32),
            pltpu.VMEM((fold + 16, LANES), f32),
            pltpu.VMEM((n_dots, 8, LANES), f32),
            pltpu.VMEM((n_dots, LANES), f32),
            pltpu.VMEM((n_col, n_dots, LANES), f32),
            pltpu.VMEM((n_row, n_dots, LANES), f32),
            pltpu.VMEM((2, rows, columns), f32),
            pltpu.VMEM((2, quarter, columns), f32),
            pltpu.VMEM((2, quarter, columns), f32),
            pltpu.VMEM((2, quarter, columns), f32),
            pltpu.VMEM((2, rows, columns), f32),
            pltpu.SemaphoreType.DMA(((2 + pairs) * tiles,)),
            pltpu.SemaphoreType.DMA((pairs * tiles + 8,)),
            pltpu.SemaphoreType.DMA((10,)),
            pltpu.SemaphoreType.DMA((10,)),
            pltpu.SemaphoreType.DMA((2, max(n_col, n_row) - 1)),
            pltpu.SemaphoreType.DMA((2, max(n_col, n_row) - 1)),
            pltpu.SemaphoreType.DMA((24,)),
            pltpu.SemaphoreType.DMA((24,)),
        ],
        compiler_params=pltpu.CompilerParams(
            collective_id=0, has_side_effects=True, vmem_limit_bytes=60 * 1024 * 1024
        ),
    )(conductance, valid_mask, focal_cells, initial_volts)


def solution(mesh):
    in_specs = (P("row", "col"), P("row", "col"), P("pair", None), P("pair", "row", "col"))
    out_specs = (P("pair", "row", "col"), P("row", "col"), P("row", "col"))
    sizes = (mesh.shape["pair"], mesh.shape["row"], mesh.shape["col"])
    return jax.shard_map(
        functools.partial(on_device, sizes), mesh=mesh, in_specs=in_specs, out_specs=out_specs, check_vma=False
    )
```

```python
import functools

import jax
import jax.numpy as jnp
from jax import lax
from jax.experimental import pallas as pl
from jax.experimental.pallas import tpu as pltpu
from jax.sharding import PartitionSpec as P

MESH = pl.DeviceIdType.MESH
LEAKAGE = 0.01
STEPS = 6
LANES = 128
EDGE = 8
OWN = 16
BLOCK = 32
PIECES = 2


def lane_ids(height):
    return lax.broadcasted_iota(jnp.int32, (height, LANES), 1)


def east(tiles):
    last = lane_ids(tiles[0].shape[0]) == LANES - 1
    rolled = [pltpu.roll(tile, LANES - 1, 1) for tile in tiles]
    return [jnp.where(last, rolled[(t + 1) % len(tiles)], rolled[t]) for t in range(len(tiles))]


def west(tiles):
    first = lane_ids(tiles[0].shape[0]) == 0
    rolled = [pltpu.roll(tile, 1, 1) for tile in tiles]
    return [jnp.where(first, rolled[t - 1], rolled[t]) for t in range(len(tiles))]


def link(a, b):
    return jnp.where(jnp.minimum(a, b) > 0.0, 0.5 * (a + b), 0.0)


def solve_coefficients(totals):
    same = [totals[2 * k] for k in range(STEPS)]
    after = [totals[2 * k + 1] for k in range(STEPS)]
    nu = [same[1], after[1]]
    for k in range(1, STEPS - 1):
        nu.append(2.0 * same[k + 1] - nu[0])
        nu.append(2.0 * after[k + 1] - nu[1])
    rho = [same[0], after[0], nu[0]]
    for k in range(1, STEPS - 2):
        rho.append(2.0 * nu[k] - rho[k])
    gram = [[None] * STEPS for _ in range(STEPS)]
    gram[0][0] = rho[0] - rho[1]
    for j in range(1, STEPS):
        gram[0][j] = rho[j] - nu[j - 1]
    for i in range(STEPS - 1):
        for j in range(i, STEPS - 1):
            before = abs(j - 1)
            gram[i + 1][j + 1] = 0.5 * (nu[i + j] + nu[abs(i - j)]) - 0.25 * (
                nu[i + j + 1] + nu[abs(i - j - 1)] + nu[i + before] + nu[abs(i - before)]
            )
    right = list(rho)
    least = [3e-7 * gram[j][j] for j in range(STEPS)]
    inverse, factors = [], {}
    for j in range(STEPS):
        pivot = gram[j][j]
        usable = pivot > least[j]
        inverse.append(jnp.where(usable, 1.0 / jnp.where(usable, pivot, 1.0), 0.0))
        for i in range(j + 1, STEPS):
            factors[i, j] = gram[j][i] * inverse[j]
        for i in range(j + 1, STEPS):
            for m in range(i, STEPS):
                gram[i][m] = gram[i][m] - factors[i, j] * gram[j][m]
            right[i] = right[i] - factors[i, j] * right[j]
    out = [right[j] * inverse[j] for j in range(STEPS)]
    for i in reversed(range(STEPS)):
        for j in range(i + 1, STEPS):
            out[i] = out[i] - factors[j, i] * out[j]
    return out


def kernel(
    sizes,
    cond_in,
    mask_in,
    focal,
    volts_in,
    volts_out,
    result_out,
    stage_cond,
    stage_mask,
    volts,
    cond,
    link_e,
    link_n,
    scale,
    coef_c,
    coef_e,
    coef_n,
    basis,
    pack_e,
    pack_w,
    land_w,
    land_e,
    dots,
    message,
    gather_col,
    gather_row,
    local,
    result,
    from_prev,
    from_next,
    far_volts,
    far_basis,
    cells,
    far_cells,
    shares,
    far_shares,
    load_sem,
    store_sem,
    halo_send,
    halo_recv,
    red_send,
    red_recv,
    far_send,
    far_recv,
    ring_send,
    ring_recv,
):
    pairs, rows, tiles, n_pair, n_row, n_col = sizes
    wide = tiles + 1
    chunks = rows // 8
    fold = rows // 4
    fold_chunks = fold // 8
    quarter = rows // 4
    unit = quarter // 4
    my_pair, my_row, my_col = lax.axis_index("pair"), lax.axis_index("row"), lax.axis_index("col")

    def around(index, step, count):
        return lax.rem(index + (step + count), count)

    loads = []
    for t in range(tiles):
        lanes = pl.ds(t * LANES, LANES)
        loads.append(pltpu.make_async_copy(cond_in.at[:, lanes], stage_cond.at[t], load_sem.at[len(loads)]))
        loads.append(pltpu.make_async_copy(mask_in.at[:, lanes], stage_mask.at[t], load_sem.at[len(loads)]))
        for p in range(pairs):
            loads.append(
                pltpu.make_async_copy(
                    volts_in.at[p, :, lanes], volts.at[p, t, pl.ds(OWN, rows)], load_sem.at[len(loads)]
                )
            )
    for load in loads:
        load.start()

    north, south = around(my_row, -1, n_row), around(my_row, 1, n_row)
    westward, eastward = around(my_col, -1, n_col), around(my_col, 1, n_col)
    partners = [{"col": around(my_col, step, n_col)} for step in range(1, n_col)]
    partners += [{"row": around(my_row, step, n_row)} for step in range(1, n_row)]
    partners += [{"row": r, "col": c} for r in (north, south) for c in (westward, eastward)]
    partners += [{"pair": around(my_pair, step, n_pair)} for step in range(1, n_pair)]
    barrier = pltpu.get_barrier_semaphore()
    for partner in partners:
        pl.semaphore_signal(barrier, inc=1, device_id=partner, device_id_type=MESH)

    zero = jnp.zeros((8, LANES), jnp.float32)
    for start in (0, rows + 3 * 8):
        at = pl.ds(start, 8)
        for t in range(wide):
            for ref in (cond, scale, link_n, coef_n):
                ref[t, at, :] = zero
            for p in range(pairs):
                volts[p, t, at, :] = zero
                for k in range(STEPS):
                    basis[k, p, t, at, :] = zero
    for start in (0, quarter + 3 * 8):
        at = pl.ds(start, 8)
        for p in range(pairs):
            for t in range(wide):
                far_volts[p, t, at, :] = zero
                for k in range(STEPS):
                    far_basis[k, p, t, at, :] = zero
    row_of = lax.broadcasted_iota(jnp.int32, (8, LANES), 0)
    packed_cells = jnp.zeros((8, LANES), jnp.int32)
    for p in range(pairs):
        for j in range(2):
            packed_cells = jnp.where(row_of == 2 * p + j, focal[p, j], packed_cells)
    cells[...] = packed_cells

    for load in loads:
        load.wait()

    def own_cond(c, carry):
        at = pl.ds(pl.multiple_of(8 * c, 8), 8)
        to = pl.ds(pl.multiple_of(OWN + 8 * c, 8), 8)
        for t in range(tiles):
            cond[t, to, :] = stage_cond[t, at, :] * stage_mask[t, at, :].astype(jnp.float32)
        return carry

    lax.fori_loop(0, chunks, own_cond, 0)

    lane = lane_ids(8)

    def pack(c, carry):
        for side, tile, ref in ((0, 0, pack_w), (1, tiles - 1, pack_e)):
            packed = jnp.zeros((8, LANES), jnp.float32)
            for g in range(4):
                at = pl.ds(pl.multiple_of(OWN + g * fold + 8 * c, 8), 8)
                fields = [volts[p, tile, at, :] for p in range(pairs)] + [cond[tile, at, :]]
                for f, value in enumerate(fields):
                    low = 32 * g + 8 * f
                    first = 0 if side == 0 else LANES - 8
                    shift = (low - first) % LANES
                    moved = pltpu.roll(value, shift, 1) if shift else value
                    packed = jnp.where((lane >= low) & (lane < low + 8), moved, packed)
            ref[pl.ds(pl.multiple_of(8 * c, 8), 8), :] = packed
        return carry

    lax.fori_loop(0, fold_chunks, pack, 0)
    pl.semaphore_wait(barrier, len(partners))

    top, bottom = pl.ds(OWN, 8), pl.ds(OWN + rows - 8, 8)
    over, under = pl.ds(OWN - 8, 8), pl.ds(OWN + rows, 8)
    mid = pl.ds(8, fold)
    halo = [
        (volts.at[:, pl.ds(0, tiles), top], volts.at[:, pl.ds(0, tiles), under], {"row": north}),
        (cond.at[pl.ds(0, tiles), top], cond.at[pl.ds(0, tiles), under], {"row": north}),
        (volts.at[:, pl.ds(0, tiles), bottom], volts.at[:, pl.ds(0, tiles), over], {"row": south}),
        (cond.at[pl.ds(0, tiles), bottom], cond.at[pl.ds(0, tiles), over], {"row": south}),
        (pack_w, land_e.at[mid], {"col": westward}),
        (pack_e, land_w.at[mid], {"col": eastward}),
        (pack_w.at[pl.ds(0, 8)], land_e.at[pl.ds(fold + 8, 8)], {"row": north, "col": westward}),
        (pack_w.at[pl.ds(fold - 8, 8)], land_e.at[pl.ds(0, 8)], {"row": south, "col": westward}),
        (pack_e.at[pl.ds(0, 8)], land_w.at[pl.ds(fold + 8, 8)], {"row": north, "col": eastward}),
        (pack_e.at[pl.ds(fold - 8, 8)], land_w.at[pl.ds(0, 8)], {"row": south, "col": eastward}),
    ]
    halo = [
        pltpu.make_async_remote_copy(
            src_ref=src,
            dst_ref=dst,
            send_sem=halo_send.at[i],
            recv_sem=halo_recv.at[i],
            device_id=who,
            device_id_type=MESH,
        )
        for i, (src, dst, who) in enumerate(halo)
    ]
    for copy in halo:
        copy.start()
    for copy in halo:
        copy.wait()

    has_n = (my_row > 0).astype(jnp.float32)
    has_s = (my_row < n_row - 1).astype(jnp.float32)
    has_w = (my_col > 0).astype(jnp.float32)
    has_e = (my_col < n_col - 1).astype(jnp.float32)
    for t in range(tiles):
        cond[t, over, :] = cond[t, over, :] * has_n
        cond[t, under, :] = cond[t, under, :] * has_s

    def unpack(source, g, to, keep):
        left = land_w[source, :]
        right = land_e[source, :]
        for f in range(pairs + 1):
            low = 32 * g + 8 * f
            a = pltpu.roll(left, (LANES - 8 - low) % LANES, 1)
            b = pltpu.roll(right, (LANES - low) % LANES, 1) if low else right
            if f == pairs:
                a, b = a * (has_w * keep), b * (has_e * keep)
            value = jnp.where(lane < 8, b, jnp.where(lane >= LANES - 8, a, 0.0))
            if f == pairs:
                cond[tiles, to, :] = value
            else:
                volts[f, tiles, to, :] = value

    def unpack_chunk(c, carry):
        for g in range(4):
            unpack(
                pl.ds(pl.multiple_of(8 + 8 * c, 8), 8),
                g,
                pl.ds(pl.multiple_of(OWN + g * fold + 8 * c, 8), 8),
                1.0,
            )
        return carry

    lax.fori_loop(0, fold_chunks, unpack_chunk, 0)
    unpack(pl.ds(0, 8), 3, over, has_n)
    unpack(pl.ds(fold + 8, 8), 0, under, has_s)

    q_next, q_prev = around(my_pair, 1, n_pair), around(my_pair, -1, n_pair)
    q_far = around(my_pair, 2, n_pair)

    def to_far(slot, src, dst):
        copy = pltpu.make_async_remote_copy(
            src_ref=src,
            dst_ref=dst,
            send_sem=far_send.at[slot],
            recv_sem=far_recv.at[slot],
            device_id={"pair": q_far},
            device_id_type=MESH,
        )
        copy.start()
        return copy

    far_rows = quarter + 2 * EDGE
    far_copies = [
        to_far(0, cells, far_cells),
        to_far(
            1,
            volts.at[:, :, pl.ds(pl.multiple_of(OWN - EDGE + q_far * quarter, 8), far_rows)],
            far_volts.at[:, :, pl.ds(8, far_rows)],
        ),
    ]

    def sweep_own(body, carry=()):
        def step(c, carry):
            return body(pl.multiple_of(OWN + BLOCK * c, 8), BLOCK, carry)

        return lax.fori_loop(0, rows // BLOCK, step, carry)

    def sweep_border(body):
        def step(i, carry):
            return body(pl.multiple_of(OWN - 8 + i * (rows + 8), 8), 8, carry)

        lax.fori_loop(0, 2, step, ())

    def links_rows(start, height, carry):
        at = pl.ds(start, height)
        here = [cond[t, at, :] for t in range(wide)]
        right = [link(a, b) for a, b in zip(here, east(here))]
        left = west(right)
        for t in range(wide):
            up = link(here[t], cond[t, pl.ds(start - 1, height), :])
            down = link(here[t], cond[t, pl.ds(start + 1, height), :])
            diagonal = up + down + left[t] + right[t] + LEAKAGE * here[t] + jnp.where(here[t] > 0.0, 0.0, 1.0)
            most = jnp.maximum(diagonal, 1.0)
            root = lax.rsqrt(most)
            root = root * (1.5 - 0.5 * most * root * root)
            link_e[t, at, :] = right[t]
            link_n[t, at, :] = up
            scale[t, at, :] = root
            coef_c[t, at, :] = 2.0 * jnp.maximum(1.0 - diagonal, 0.0)
        return carry

    sweep_border(links_rows)
    sweep_own(links_rows)

    width_all = tiles * LANES * n_col

    def coefficient_rows(start, height, carry):
        at = pl.ds(start, height)
        root = [scale[t, at, :] for t in range(wide)]
        root_e = east(root)
        for t in range(wide):
            coef_e[t, at, :] = 2.0 * link_e[t, at, :] * root[t] * root_e[t]
            coef_n[t, at, :] = 2.0 * link_n[t, at, :] * root[t] * scale[t, pl.ds(start - 1, height), :]
        return carry

    def start_rows(field, out, ids, shift, start, height, carry):
        at, up_at, down_at = pl.ds(start, height), pl.ds(start - 1, height), pl.ds(start + 1, height)
        base = pl.multiple_of(start + shift, 8)
        own_at = pl.ds(base, height)
        column = lane_ids(height)
        sub = lax.broadcasted_iota(jnp.int32, (height, LANES), 0)
        first = my_col * (tiles * LANES)
        columns = [first + t * LANES + column for t in range(tiles)]
        columns.append(first + jnp.where(column < 64, tiles * LANES, -LANES) + column)
        right = [link_e[t, own_at, :] for t in range(wide)]
        flat = (my_row * rows + base - OWN + sub) * width_all
        own = []
        for t in range(wide):
            value = cond[t, own_at, :]
            own.append(LEAKAGE * value + jnp.where(value > 0.0, 0.0, 1.0))
        for p in range(pairs):
            here = [field[p, t, at, :] for t in range(wide)]
            there = east(here)
            flow = [right[t] * (here[t] - there[t]) for t in range(wide)]
            flow_w = west(flow)
            for t in range(wide):
                total = flow[t] - flow_w[t] + own[t] * here[t]
                total = total + link_n[t, own_at, :] * (here[t] - field[p, t, up_at, :])
                total = total + link_n[t, pl.ds(base + 1, height), :] * (here[t] - field[p, t, down_at, :])
                cell = flat + columns[t]
                inject = jnp.where(cell == ids[2 * p], 1.0, 0.0) - jnp.where(cell == ids[2 * p + 1], 1.0, 0.0)
                out[0, p, t, at, :] = scale[t, own_at, :] * (inject - total)
        return carry

    sweep_border(coefficient_rows)
    sweep_own(coefficient_rows)
    start_own = functools.partial(
        start_rows, volts, basis, [focal[p, j] for p in range(pairs) for j in range(2)], 0
    )
    sweep_border(start_own)
    sweep_own(start_own)

    def advance(basis, shift, k, start, height, sums):
        at, up_at, down_at = pl.ds(start, height), pl.ds(start - 1, height), pl.ds(start + 1, height)
        base = pl.multiple_of(start + shift, 8)
        own_at = pl.ds(base, height)
        final = k == STEPS - 1
        count = tiles if final else wide
        right = [coef_e[t, own_at, :] for t in range(wide)]
        out = []
        for p in range(pairs):
            here = [basis[k, p, t, at, :] for t in range(wide)]
            there = east(here)
            back = west([right[t] * here[t] for t in range(wide)])
            same = jnp.zeros((height, LANES), jnp.float32)
            step = jnp.zeros((height, LANES), jnp.float32)
            for t in range(count):
                value = coef_c[t, own_at, :] * here[t] + right[t] * there[t] + back[t]
                value = value + coef_n[t, own_at, :] * basis[k, p, t, up_at, :]
                value = value + coef_n[t, pl.ds(base + 1, height), :] * basis[k, p, t, down_at, :]
                value = 0.5 * value if k < 2 else value - basis[k - 1, p, t, at, :]
                if not final:
                    basis[k + 1, p, t, at, :] = value
                if sums and t < tiles:
                    same = same + here[t] * here[t]
                    step = step + here[t] * value
            if sums:
                out += [sums[2 * p] + same, sums[2 * p + 1] + step]
        return tuple(out) if sums else sums

    def fold_rows(value):
        total = value[:8]
        for i in range(1, BLOCK // 8):
            total = total + value[8 * i : 8 * i + 8]
        return total

    for k in range(STEPS):
        if k < STEPS - 1:
            sweep_border(functools.partial(advance, basis, 0, k))
        tall_zero = jnp.zeros((BLOCK, LANES), jnp.float32)
        sums = sweep_own(functools.partial(advance, basis, 0, k), (tall_zero,) * (2 * pairs))
        for p in range(pairs):
            dots[(2 * k) * pairs + p] = fold_rows(sums[2 * p])
            dots[(2 * k + 1) * pairs + p] = fold_rows(sums[2 * p + 1])

    n_dots = 2 * STEPS * pairs
    part = jnp.sum(dots[...], axis=1)
    message[...] = jnp.broadcast_to(jnp.sum(part, axis=1, keepdims=True), (n_dots, LANES))

    def reduce_over(axis, me, count, source, gather, phase):
        copies = []
        for step in range(1, count):
            copies.append(
                pltpu.make_async_remote_copy(
                    src_ref=source,
                    dst_ref=gather.at[me],
                    send_sem=red_send.at[phase, step - 1],
                    recv_sem=red_recv.at[phase, step - 1],
                    device_id={axis: around(me, step, count)},
                    device_id_type=MESH,
                )
            )
        for copy in copies:
            copy.start()
        gather[me] = source[...]
        for copy in copies:
            copy.wait()
        total = gather[0]
        for i in range(1, count):
            total = total + gather[i]
        return total

    message[...] = reduce_over("col", my_col, n_col, message, gather_col, 0)
    totals = reduce_over("row", my_row, n_row, message, gather_row, 1)
    parts = solve_coefficients([totals[j * pairs : (j + 1) * pairs] for j in range(2 * STEPS)])
    for k in range(STEPS):
        shares[pl.ds(k * pairs, pairs), :] = parts[k]
    far_copies.append(to_far(2, shares, far_shares))

    def volts_rows(field, basis, shares, shift, start, height, carry):
        at = pl.ds(start, height)
        for p in range(pairs):
            for t in range(wide):
                change = shares[pl.ds(p, 1), :] * basis[0, p, t, at, :]
                for k in range(1, STEPS):
                    change = change + shares[pl.ds(k * pairs + p, 1), :] * basis[k, p, t, at, :]
                value = field[p, t, at, :] + scale[t, pl.ds(pl.multiple_of(start + shift, 8), height), :] * change
                field[p, t, at, :] = value
        return carry

    far_copies[1].wait_send()
    sweep_border(functools.partial(volts_rows, volts, basis, shares, 0))
    sweep_own(functools.partial(volts_rows, volts, basis, shares, 0))
    stores = []
    for t in range(tiles):
        for p in range(pairs):
            stores.append(
                pltpu.make_async_copy(
                    volts.at[p, t, pl.ds(OWN, rows)],
                    volts_out.at[p, :, pl.ds(t * LANES, LANES)],
                    store_sem.at[len(stores)],
                )
            )


    def currents(index, i, fields):
        row = index * quarter + BLOCK * i
        start = pl.multiple_of(OWN + row, 8)
        right = [link_e[t, pl.ds(start, BLOCK), :] for t in range(wide)]
        total, peak = [None] * tiles, [None] * tiles
        for field, first in fields:
            at, up_at, down_at = pl.ds(first, BLOCK), pl.ds(first - 1, BLOCK), pl.ds(first + 1, BLOCK)
            for p in range(pairs):
                here = [field[p, t, at, :] for t in range(wide)]
                there = east(here)
                flow = [jnp.abs(right[t] * (here[t] - there[t])) for t in range(wide)]
                flow_w = west(flow)
                for t in range(tiles):
                    value = flow[t] + flow_w[t]
                    value = value + jnp.abs(link_n[t, pl.ds(start, BLOCK), :] * (here[t] - field[p, t, up_at, :]))
                    value = value + jnp.abs(
                        link_n[t, pl.ds(start + 1, BLOCK), :] * (here[t] - field[p, t, down_at, :])
                    )
                    value = 0.5 * value
                    total[t] = value if total[t] is None else total[t] + value
                    peak[t] = value if peak[t] is None else jnp.maximum(peak[t], value)
        to = pl.ds(pl.multiple_of(row, 8), BLOCK)
        for t in range(tiles):
            local[0, to, pl.ds(t * LANES, LANES)] = total[t]
            local[1, to, pl.ds(t * LANES, LANES)] = peak[t]

    def span(index, u):
        return pl.ds(pl.multiple_of(index * quarter + u * unit, unit), unit)

    def ring(slot, src, dst, who):
        copy = pltpu.make_async_remote_copy(
            src_ref=src,
            dst_ref=dst,
            send_sem=ring_send.at[slot],
            recv_sem=ring_recv.at[slot],
            device_id={"pair": who},
            device_id_type=MESH,
        )
        copy.start()
        return copy

    in_unit = [pl.ds(u * unit, unit) for u in range(4)]
    in_block = BLOCK // unit
    sent = {}
    for i in range(quarter // BLOCK):
        for owner, name, base, target in ((q_next, "prev", 0, from_prev), (q_prev, "next", 4, from_next)):
            currents(owner, i, [(volts, pl.multiple_of(OWN + owner * quarter + BLOCK * i, 8))])
            for u in range(i * in_block, (i + 1) * in_block):
                sent[name, u] = ring(base + u, local.at[:, span(owner, u)], target.at[:, in_unit[u]], owner)

    for store in stores:
        store.start()

    far_copies[0].wait_recv()
    far_copies[1].wait_recv()
    shift = my_pair * quarter
    half = far_rows // 2

    def sweep_far(body):
        def step(c, carry):
            return body(pl.multiple_of(8 + half * c, 8), half, carry)

        lax.fori_loop(0, 2, step, ())

    sweep_far(
        functools.partial(
            start_rows, far_volts, far_basis, [far_cells[pl.ds(r, 1), :] for r in range(2 * pairs)], shift
        )
    )
    for k in range(STEPS - 1):
        sweep_far(functools.partial(advance, far_basis, shift, k))
    far_copies[2].wait_recv()
    sweep_far(functools.partial(volts_rows, far_volts, far_basis, far_shares, shift))

    for i in range(quarter // BLOCK):
        currents(
            my_pair,
            i,
            [
                (volts, pl.multiple_of(OWN + my_pair * quarter + BLOCK * i, 8)),
                (far_volts, OWN + BLOCK * i),
            ],
        )
    for u in range(4):
        sent["prev", u].wait_recv()
        sent["next", u].wait_recv()
        at = span(my_pair, u)
        result[0, at, :] = local[0, at, :] + from_prev[0, in_unit[u], :] + from_next[0, in_unit[u], :]
        result[1, at, :] = jnp.maximum(
            local[1, at, :], jnp.maximum(from_prev[1, in_unit[u], :], from_next[1, in_unit[u], :])
        )
        sent["up", u] = ring(8 + u, result.at[:, at], result.at[:, at], q_next)
        sent["down", u] = ring(12 + u, result.at[:, at], result.at[:, at], q_prev)

    def keep(index, slot, first, count):
        at = pl.ds(pl.multiple_of(index * quarter + first * unit, unit), count * unit)
        stores.append(pltpu.make_async_copy(result.at[:, at], result_out.at[:, at], store_sem.at[pairs * tiles + slot]))
        stores[-1].start()

    for i in range(2):
        sent["up", i].wait_recv()
        at = span(q_prev, i)
        sent["over", i] = ring(16 + i, result.at[:, at], result.at[:, at], q_next)
        sent["down", 2 + i].wait_recv()
        at = span(q_next, 2 + i)
        sent["over", 2 + i] = ring(18 + i, result.at[:, at], result.at[:, at], q_prev)
    keep(my_pair, 0, 0, 4)
    for i in range(2):
        sent["up", 2 + i].wait_recv()
        sent["down", i].wait_recv()
    keep(q_prev, 1, 0, 4)
    keep(q_next, 2, 0, 4)
    for i in range(2):
        sent["over", i].wait_recv()
        sent["over", 2 + i].wait_recv()
        keep(q_far, 3 + 2 * i, i, 1)
        keep(q_far, 4 + 2 * i, 2 + i, 1)
    for copy in sent.values():
        copy.wait_send()
    far_copies[0].wait_send()
    far_copies[2].wait_send()
    for store in stores:
        store.wait()


def write_out(volts, result, volts_out, sum_out, max_out, held_volts, held_result, load_sem, store_sem):
    pairs, rows = volts.shape[:2]
    part = rows // PIECES
    loads, stores = [], []
    for i in range(PIECES):
        at = pl.ds(i * part, part)
        moves = [(volts.at[p, at], held_volts.at[p, at], volts_out.at[p, at]) for p in range(pairs)]
        moves.append((result.at[0, at], held_result.at[0, at], sum_out.at[at]))
        moves.append((result.at[1, at], held_result.at[1, at], max_out.at[at]))
        for src, held, dst in moves:
            n = len(loads)
            loads.append(pltpu.make_async_copy(src, held, load_sem.at[n]))
            stores.append(pltpu.make_async_copy(held, dst, store_sem.at[n]))
    for load in loads:
        load.start()
    for load, store in zip(loads, stores):
        load.wait()
        store.start()
    for store in stores:
        store.wait()


def on_device(mesh_sizes, conductance, valid_mask, focal_cells, initial_volts):
    rows, columns = conductance.shape
    pairs = initial_volts.shape[0]
    tiles = columns // LANES
    n_pair, n_row, n_col = mesh_sizes
    sizes = (pairs, rows, tiles, n_pair, n_row, n_col)
    wide, tall, fold, quarter = tiles + 1, rows + 32, rows // 4, rows // 4
    n_dots = 2 * STEPS * pairs
    f32 = jnp.float32
    stay = pl.BlockSpec(memory_space=pltpu.HBM)
    raster = pltpu.VMEM((wide, tall, LANES), f32)
    volts, result = pl.pallas_call(
        functools.partial(kernel, sizes),
        out_shape=(
            jax.ShapeDtypeStruct((pairs, rows, columns), f32),
            jax.ShapeDtypeStruct((2, rows, columns), f32),
        ),
        in_specs=[stay, stay, pl.BlockSpec(memory_space=pltpu.SMEM), stay],
        out_specs=(stay, stay),
        scratch_shapes=[
            pltpu.VMEM((tiles, rows, LANES), f32),
            pltpu.VMEM((tiles, rows, LANES), jnp.int32),
            pltpu.VMEM((pairs, wide, tall, LANES), f32),
            raster,
            raster,
            raster,
            raster,
            raster,
            raster,
            raster,
            pltpu.VMEM((STEPS, pairs, wide, tall, LANES), f32),
            pltpu.VMEM((fold, LANES), f32),
            pltpu.VMEM((fold, LANES), f32),
            pltpu.VMEM((fold + 16, LANES), f32),
            pltpu.VMEM((fold + 16, LANES), f32),
            pltpu.VMEM((n_dots, 8, LANES), f32),
            pltpu.VMEM((n_dots, LANES), f32),
            pltpu.VMEM((n_col, n_dots, LANES), f32),
            pltpu.VMEM((n_row, n_dots, LANES), f32),
            pltpu.VMEM((2, rows, columns), f32),
            pltpu.VMEM((2, rows, columns), f32),
            pltpu.VMEM((2, quarter, columns), f32),
            pltpu.VMEM((2, quarter, columns), f32),
            pltpu.VMEM((pairs, wide, quarter + 32, LANES), f32),
            pltpu.VMEM((STEPS, pairs, wide, quarter + 32, LANES), f32),
            pltpu.VMEM((8, LANES), jnp.int32),
            pltpu.VMEM((8, LANES), jnp.int32),
            pltpu.VMEM((8 * ((STEPS * pairs + 7) // 8), LANES), f32),
            pltpu.VMEM((8 * ((STEPS * pairs + 7) // 8), LANES), f32),
            pltpu.SemaphoreType.DMA(((2 + pairs) * tiles,)),
            pltpu.SemaphoreType.DMA((pairs * tiles + 7,)),
            pltpu.SemaphoreType.DMA((10,)),
            pltpu.SemaphoreType.DMA((10,)),
            pltpu.SemaphoreType.DMA((2, max(n_col, n_row) - 1)),
            pltpu.SemaphoreType.DMA((2, max(n_col, n_row) - 1)),
            pltpu.SemaphoreType.DMA((3,)),
            pltpu.SemaphoreType.DMA((3,)),
            pltpu.SemaphoreType.DMA((20,)),
            pltpu.SemaphoreType.DMA((20,)),
        ],
        compiler_params=pltpu.CompilerParams(
            collective_id=0, has_side_effects=True, vmem_limit_bytes=int(61 * 1024 * 1024)
        ),
    )(conductance, valid_mask, focal_cells, initial_volts)
    flat = jax.ShapeDtypeStruct((rows, columns), f32)
    return pl.pallas_call(
        write_out,
        out_shape=(jax.ShapeDtypeStruct((pairs, rows, columns), f32), flat, flat),
        in_specs=[stay, stay],
        out_specs=(stay, stay, stay),
        scratch_shapes=[
            pltpu.VMEM((pairs, rows, columns), f32),
            pltpu.VMEM((2, rows, columns), f32),
            pltpu.SemaphoreType.DMA((PIECES * (pairs + 2),)),
            pltpu.SemaphoreType.DMA((PIECES * (pairs + 2),)),
        ],
    )(volts, result)


def solution(mesh):
    in_specs = (P("row", "col"), P("row", "col"), P("pair", None), P("pair", "row", "col"))
    out_specs = (P("pair", "row", "col"), P("row", "col"), P("row", "col"))
    sizes = (mesh.shape["pair"], mesh.shape["row"], mesh.shape["col"])
    return jax.shard_map(
        functools.partial(on_device, sizes), mesh=mesh, in_specs=in_specs, out_specs=out_specs, check_vma=False
    )
```

```python
import functools

import jax
import jax.numpy as jnp
from jax import lax
from jax.experimental import pallas as pl
from jax.experimental.pallas import tpu as pltpu
from jax.sharding import PartitionSpec as P

MESH = pl.DeviceIdType.MESH
LEAKAGE = 0.01
STEPS = 6
LANES = 128
EDGE = 8
OWN = 16
BLOCK = 32
SWEEP = 64
HALF_BLOCK = 16
NEAR_EARLY = 1
PIECES = 2


def lane_ids(height):
    return lax.broadcasted_iota(jnp.int32, (height, LANES), 1)


def east(tiles):
    last = lane_ids(tiles[0].shape[0]) == LANES - 1
    rolled = [pltpu.roll(tile, LANES - 1, 1) for tile in tiles]
    return [jnp.where(last, rolled[(t + 1) % len(tiles)], rolled[t]) for t in range(len(tiles))]


def west(tiles):
    first = lane_ids(tiles[0].shape[0]) == 0
    rolled = [pltpu.roll(tile, 1, 1) for tile in tiles]
    return [jnp.where(first, rolled[t - 1], rolled[t]) for t in range(len(tiles))]


def link(a, b):
    return jnp.where(jnp.minimum(a, b) > 0.0, 0.5 * (a + b), 0.0)


def solve_coefficients(totals):
    same = [totals[2 * k] for k in range(STEPS)]
    after = [totals[2 * k + 1] for k in range(STEPS)]
    nu = [same[1], after[1]]
    for k in range(1, STEPS - 1):
        nu.append(2.0 * same[k + 1] - nu[0])
        nu.append(2.0 * after[k + 1] - nu[1])
    rho = [same[0], after[0], nu[0]]
    for k in range(1, STEPS - 2):
        rho.append(2.0 * nu[k] - rho[k])
    gram = [[None] * STEPS for _ in range(STEPS)]
    gram[0][0] = rho[0] - rho[1]
    for j in range(1, STEPS):
        gram[0][j] = rho[j] - nu[j - 1]
    for i in range(STEPS - 1):
        for j in range(i, STEPS - 1):
            before = abs(j - 1)
            gram[i + 1][j + 1] = 0.5 * (nu[i + j] + nu[abs(i - j)]) - 0.25 * (
                nu[i + j + 1] + nu[abs(i - j - 1)] + nu[i + before] + nu[abs(i - before)]
            )
    right = list(rho)
    least = [3e-7 * gram[j][j] for j in range(STEPS)]
    inverse, factors = [], {}
    for j in range(STEPS):
        pivot = gram[j][j]
        usable = pivot > least[j]
        inverse.append(jnp.where(usable, 1.0 / jnp.where(usable, pivot, 1.0), 0.0))
        for i in range(j + 1, STEPS):
            factors[i, j] = gram[j][i] * inverse[j]
        for i in range(j + 1, STEPS):
            for m in range(i, STEPS):
                gram[i][m] = gram[i][m] - factors[i, j] * gram[j][m]
            right[i] = right[i] - factors[i, j] * right[j]
    out = [right[j] * inverse[j] for j in range(STEPS)]
    for i in reversed(range(STEPS)):
        for j in range(i + 1, STEPS):
            out[i] = out[i] - factors[j, i] * out[j]
    return out


def kernel(
    sizes,
    cond_in,
    mask_in,
    focal,
    volts_in,
    volts_out,
    result_out,
    stage_cond,
    stage_mask,
    volts,
    cond,
    link_e,
    link_n,
    scale,
    coef_c,
    coef_e,
    coef_n,
    basis,
    pack_e,
    pack_w,
    land_w,
    land_e,
    dots,
    message,
    gather_col,
    gather_row,
    result,
    late,
    late_prev,
    late_next,
    far_volts,
    far_basis,
    far_pack,
    land_pack,
    cells,
    far_cells,
    shares,
    far_shares,
    load_sem,
    store_sem,
    halo_send,
    halo_recv,
    red_send,
    red_recv,
    far_send,
    far_recv,
    ring_send,
    ring_recv,
):
    pairs, rows, tiles, n_pair, n_row, n_col = sizes
    wide = tiles + 1
    chunks = rows // 8
    fold = rows // 4
    fold_chunks = fold // 8
    quarter = rows // 4
    unit = quarter // 4
    my_pair, my_row, my_col = lax.axis_index("pair"), lax.axis_index("row"), lax.axis_index("col")

    def around(index, step, count):
        return lax.rem(index + (step + count), count)

    loads = []
    for t in range(tiles):
        lanes = pl.ds(t * LANES, LANES)
        loads.append(pltpu.make_async_copy(cond_in.at[:, lanes], stage_cond.at[t], load_sem.at[len(loads)]))
        loads.append(pltpu.make_async_copy(mask_in.at[:, lanes], stage_mask.at[t], load_sem.at[len(loads)]))
        for p in range(pairs):
            loads.append(
                pltpu.make_async_copy(
                    volts_in.at[p, :, lanes], volts.at[p, t, pl.ds(OWN, rows)], load_sem.at[len(loads)]
                )
            )
    for load in loads:
        load.start()

    north, south = around(my_row, -1, n_row), around(my_row, 1, n_row)
    westward, eastward = around(my_col, -1, n_col), around(my_col, 1, n_col)
    partners = [{"col": around(my_col, step, n_col)} for step in range(1, n_col)]
    partners += [{"row": around(my_row, step, n_row)} for step in range(1, n_row)]
    partners += [{"row": r, "col": c} for r in (north, south) for c in (westward, eastward)]
    partners += [{"pair": around(my_pair, step, n_pair)} for step in range(1, n_pair)]
    barrier = pltpu.get_barrier_semaphore()
    for partner in partners:
        pl.semaphore_signal(barrier, inc=1, device_id=partner, device_id_type=MESH)

    zero = jnp.zeros((8, LANES), jnp.float32)
    for start in (0, rows + 3 * 8):
        at = pl.ds(start, 8)
        for t in range(wide):
            for ref in (cond, scale, link_n, coef_n):
                ref[t, at, :] = zero
            for p in range(pairs):
                volts[p, t, at, :] = zero
                for k in range(STEPS):
                    basis[k, p, t, at, :] = zero
    for start in (0, quarter + 3 * 8):
        at = pl.ds(start, 8)
        for s in range(n_pair - 1):
            for p in range(pairs):
                for t in range(wide):
                    far_volts[s, p, t, at, :] = zero
                    for k in range(STEPS):
                        far_basis[s, k, p, t, at, :] = zero
    row_of = lax.broadcasted_iota(jnp.int32, (8, LANES), 0)
    packed_cells = jnp.zeros((8, LANES), jnp.int32)
    for p in range(pairs):
        for j in range(2):
            packed_cells = jnp.where(row_of == 2 * p + j, focal[p, j], packed_cells)
    cells[...] = packed_cells

    for load in loads:
        load.wait()

    def own_cond(c, carry):
        at = pl.ds(pl.multiple_of(8 * c, 8), 8)
        to = pl.ds(pl.multiple_of(OWN + 8 * c, 8), 8)
        for t in range(tiles):
            cond[t, to, :] = stage_cond[t, at, :] * stage_mask[t, at, :].astype(jnp.float32)
        return carry

    lax.fori_loop(0, chunks, own_cond, 0)

    lane = lane_ids(8)

    def pack(c, carry):
        for side, tile, ref in ((0, 0, pack_w), (1, tiles - 1, pack_e)):
            packed = jnp.zeros((8, LANES), jnp.float32)
            for g in range(4):
                at = pl.ds(pl.multiple_of(OWN + g * fold + 8 * c, 8), 8)
                fields = [volts[p, tile, at, :] for p in range(pairs)] + [cond[tile, at, :]]
                for f, value in enumerate(fields):
                    low = 32 * g + 8 * f
                    first = 0 if side == 0 else LANES - 8
                    shift = (low - first) % LANES
                    moved = pltpu.roll(value, shift, 1) if shift else value
                    packed = jnp.where((lane >= low) & (lane < low + 8), moved, packed)
            ref[pl.ds(pl.multiple_of(8 * c, 8), 8), :] = packed
        return carry

    lax.fori_loop(0, fold_chunks, pack, 0)
    pl.semaphore_wait(barrier, len(partners))

    top, bottom = pl.ds(OWN, 8), pl.ds(OWN + rows - 8, 8)
    over, under = pl.ds(OWN - 8, 8), pl.ds(OWN + rows, 8)
    mid = pl.ds(8, fold)
    halo = [
        (volts.at[:, pl.ds(0, tiles), top], volts.at[:, pl.ds(0, tiles), under], {"row": north}),
        (cond.at[pl.ds(0, tiles), top], cond.at[pl.ds(0, tiles), under], {"row": north}),
        (volts.at[:, pl.ds(0, tiles), bottom], volts.at[:, pl.ds(0, tiles), over], {"row": south}),
        (cond.at[pl.ds(0, tiles), bottom], cond.at[pl.ds(0, tiles), over], {"row": south}),
        (pack_w, land_e.at[mid], {"col": westward}),
        (pack_e, land_w.at[mid], {"col": eastward}),
        (pack_w.at[pl.ds(0, 8)], land_e.at[pl.ds(fold + 8, 8)], {"row": north, "col": westward}),
        (pack_w.at[pl.ds(fold - 8, 8)], land_e.at[pl.ds(0, 8)], {"row": south, "col": westward}),
        (pack_e.at[pl.ds(0, 8)], land_w.at[pl.ds(fold + 8, 8)], {"row": north, "col": eastward}),
        (pack_e.at[pl.ds(fold - 8, 8)], land_w.at[pl.ds(0, 8)], {"row": south, "col": eastward}),
    ]
    halo = [
        pltpu.make_async_remote_copy(
            src_ref=src,
            dst_ref=dst,
            send_sem=halo_send.at[i],
            recv_sem=halo_recv.at[i],
            device_id=who,
            device_id_type=MESH,
        )
        for i, (src, dst, who) in enumerate(halo)
    ]
    for copy in halo:
        copy.start()

    ahead = (1, n_pair - 1, 2)
    owners = [around(my_pair, step, n_pair) for step in ahead]
    early = (min(NEAR_EARLY, pairs), min(NEAR_EARLY, pairs), pairs)
    moves = {}

    def give(s, kind, src, dst):
        slot = 5 * s + len([key for key in moves if key[0] == s])
        moves[s, kind] = pltpu.make_async_remote_copy(
            src_ref=src,
            dst_ref=dst,
            send_sem=far_send.at[slot],
            recv_sem=far_recv.at[slot],
            device_id={"pair": owners[s]},
            device_id_type=MESH,
        )
        moves[s, kind].start()

    def give_main(s):
        if not early[s]:
            return
        start = pl.multiple_of(OWN + owners[s] * quarter, 8)
        give(
            s,
            "main",
            volts.at[pl.ds(0, early[s]), pl.ds(0, tiles), pl.ds(start, quarter)],
            far_volts.at[s, pl.ds(0, early[s]), pl.ds(0, tiles), pl.ds(OWN, quarter)],
        )

    def give_border(s):
        if not early[s]:
            return
        start = OWN + owners[s] * quarter
        for kind, offset in (("over", -EDGE), ("under", quarter)):
            give(
                s,
                kind,
                volts.at[pl.ds(0, early[s]), pl.ds(0, tiles), pl.ds(pl.multiple_of(start + offset, 8), EDGE)],
                far_volts.at[s, pl.ds(0, early[s]), pl.ds(0, tiles), pl.ds(OWN + offset, EDGE)],
            )
        give(s, "pack", far_pack.at[s], land_pack.at[s])
        give(s, "cells", cells, far_cells.at[s])

    give_main(0)
    give_main(1)
    give_main(2)
    for copy in halo:
        copy.wait()

    has_n = (my_row > 0).astype(jnp.float32)
    has_s = (my_row < n_row - 1).astype(jnp.float32)
    has_w = (my_col > 0).astype(jnp.float32)
    has_e = (my_col < n_col - 1).astype(jnp.float32)
    for t in range(tiles):
        cond[t, over, :] = cond[t, over, :] * has_n
        cond[t, under, :] = cond[t, under, :] * has_s

    def unpack(source, g, to, keep):
        left = land_w[source, :]
        right = land_e[source, :]
        for f in range(pairs + 1):
            low = 32 * g + 8 * f
            a = pltpu.roll(left, (LANES - 8 - low) % LANES, 1)
            b = pltpu.roll(right, (LANES - low) % LANES, 1) if low else right
            if f == pairs:
                a, b = a * (has_w * keep), b * (has_e * keep)
            value = jnp.where(lane < 8, b, jnp.where(lane >= LANES - 8, a, 0.0))
            if f == pairs:
                cond[tiles, to, :] = value
            else:
                volts[f, tiles, to, :] = value

    def unpack_chunk(c, carry):
        for g in range(4):
            unpack(
                pl.ds(pl.multiple_of(8 + 8 * c, 8), 8),
                g,
                pl.ds(pl.multiple_of(OWN + g * fold + 8 * c, 8), 8),
                1.0,
            )
        return carry

    lax.fori_loop(0, fold_chunks, unpack_chunk, 0)
    unpack(pl.ds(0, 8), 3, over, has_n)
    unpack(pl.ds(fold + 8, 8), 0, under, has_s)

    far_rows = quarter + 2 * EDGE

    def pack_place(j, p):
        return 32 * (j % 4) + 16 * p

    for s in range(n_pair - 1):
        start = OWN - EDGE + owners[s] * quarter
        for c in range(far_pack.shape[1] // 8):
            packed = jnp.zeros((8, LANES), jnp.float32)
            for j in range(4 * c, min(4 * c + 4, far_rows // 8)):
                for p in range(early[s]):
                    low = pack_place(j, p)
                    value = volts[p, tiles, pl.ds(pl.multiple_of(start + 8 * j, 8), 8), :]
                    moved = pltpu.roll(value, (low + 8) % LANES, 1)
                    packed = jnp.where((lane >= low) & (lane < low + 16), moved, packed)
            far_pack[s, pl.ds(8 * c, 8), :] = packed
    give_border(0)
    give_border(1)
    give_border(2)

    def take(s):
        for kind in ("main", "over", "under", "pack", "cells"):
            moves[s, kind].wait_recv()
        for j in range(far_rows // 8):
            for p in range(early[s]):
                moved = pltpu.roll(
                    land_pack[s, pl.ds(8 * (j // 4), 8), :], (2 * LANES - 8 - pack_place(j, p)) % LANES, 1
                )
                far_volts[s, p, tiles, pl.ds(8 + 8 * j, 8), :] = jnp.where(
                    (lane < 8) | (lane >= LANES - 8), moved, 0.0
                )

    def sweep_own(body, carry=(), height=BLOCK):
        def step(c, carry):
            return body(pl.multiple_of(OWN + height * c, 8), height, carry)

        return lax.fori_loop(0, rows // height, step, carry)

    def sweep_border(body):
        def step(i, carry):
            return body(pl.multiple_of(OWN - 8 + i * (rows + 8), 8), 8, carry)

        lax.fori_loop(0, 2, step, ())

    def links_rows(start, height, carry):
        at = pl.ds(start, height)
        here = [cond[t, at, :] for t in range(wide)]
        right = [link(a, b) for a, b in zip(here, east(here))]
        left = west(right)
        for t in range(wide):
            up = link(here[t], cond[t, pl.ds(start - 1, height), :])
            down = link(here[t], cond[t, pl.ds(start + 1, height), :])
            diagonal = up + down + left[t] + right[t] + LEAKAGE * here[t] + jnp.where(here[t] > 0.0, 0.0, 1.0)
            most = jnp.maximum(diagonal, 1.0)
            root = lax.rsqrt(most)
            root = root * (1.5 - 0.5 * most * root * root)
            link_e[t, at, :] = right[t]
            link_n[t, at, :] = up
            scale[t, at, :] = root
            coef_c[t, at, :] = 2.0 * jnp.maximum(1.0 - diagonal, 0.0)
        return carry

    sweep_border(links_rows)
    sweep_own(links_rows)

    width_all = tiles * LANES * n_col

    def coefficient_rows(start, height, carry):
        at = pl.ds(start, height)
        root = [scale[t, at, :] for t in range(wide)]
        root_e = east(root)
        for t in range(wide):
            coef_e[t, at, :] = 2.0 * link_e[t, at, :] * root[t] * root_e[t]
            coef_n[t, at, :] = 2.0 * link_n[t, at, :] * root[t] * scale[t, pl.ds(start - 1, height), :]
        return carry

    def start_rows(count, field, out, ids, shift, start, height, carry):
        at, up_at, down_at = pl.ds(start, height), pl.ds(start - 1, height), pl.ds(start + 1, height)
        base = pl.multiple_of(start + shift, 8)
        own_at = pl.ds(base, height)
        column = lane_ids(height)
        sub = lax.broadcasted_iota(jnp.int32, (height, LANES), 0)
        first = my_col * (tiles * LANES)
        columns = [first + t * LANES + column for t in range(tiles)]
        columns.append(first + jnp.where(column < 64, tiles * LANES, -LANES) + column)
        right = [link_e[t, own_at, :] for t in range(wide)]
        flat = (my_row * rows + base - OWN + sub) * width_all
        own = []
        for t in range(wide):
            value = cond[t, own_at, :]
            own.append(LEAKAGE * value + jnp.where(value > 0.0, 0.0, 1.0))
        for p in range(count):
            here = [field[p, t, at, :] for t in range(wide)]
            there = east(here)
            flow = [right[t] * (here[t] - there[t]) for t in range(wide)]
            flow_w = west(flow)
            for t in range(wide):
                total = flow[t] - flow_w[t] + own[t] * here[t]
                total = total + link_n[t, own_at, :] * (here[t] - field[p, t, up_at, :])
                total = total + link_n[t, pl.ds(base + 1, height), :] * (here[t] - field[p, t, down_at, :])
                cell = flat + columns[t]
                inject = jnp.where(cell == ids[2 * p], 1.0, 0.0) - jnp.where(cell == ids[2 * p + 1], 1.0, 0.0)
                out[0, p, t, at, :] = scale[t, own_at, :] * (inject - total)
        return carry

    sweep_border(coefficient_rows)
    sweep_own(coefficient_rows)
    start_own = functools.partial(
        start_rows, pairs, volts, basis, [focal[p, j] for p in range(pairs) for j in range(2)], 0
    )
    sweep_border(start_own)
    sweep_own(start_own)

    def advance(fields, basis, shift, k, start, height, sums):
        at, up_at, down_at = pl.ds(start, height), pl.ds(start - 1, height), pl.ds(start + 1, height)
        base = pl.multiple_of(start + shift, 8)
        own_at = pl.ds(base, height)
        final = k == STEPS - 1
        count = tiles if final else wide
        right = [coef_e[t, own_at, :] for t in range(wide)]
        out = []
        for p in range(fields):
            here = [basis[k, p, t, at, :] for t in range(wide)]
            there = east(here)
            back = west([right[t] * here[t] for t in range(wide)])
            same = jnp.zeros((height, LANES), jnp.float32)
            step = jnp.zeros((height, LANES), jnp.float32)
            for t in range(count):
                value = coef_c[t, own_at, :] * here[t] + right[t] * there[t] + back[t]
                value = value + coef_n[t, own_at, :] * basis[k, p, t, up_at, :]
                value = value + coef_n[t, pl.ds(base + 1, height), :] * basis[k, p, t, down_at, :]
                value = 0.5 * value if k < 2 else value - basis[k - 1, p, t, at, :]
                if not final:
                    basis[k + 1, p, t, at, :] = value
                if sums and t < tiles:
                    same = same + here[t] * here[t]
                    step = step + here[t] * value
            if sums:
                out += [sums[2 * p] + same, sums[2 * p + 1] + step]
        return tuple(out) if sums else sums

    def fold_rows(value):
        total = value[:8]
        for i in range(1, SWEEP // 8):
            total = total + value[8 * i : 8 * i + 8]
        return total

    for k in range(STEPS):
        if k < STEPS - 1:
            sweep_border(functools.partial(advance, pairs, basis, 0, k))
        tall_zero = jnp.zeros((SWEEP, LANES), jnp.float32)
        sums = sweep_own(functools.partial(advance, pairs, basis, 0, k), (tall_zero,) * (2 * pairs), SWEEP)
        for p in range(pairs):
            dots[(2 * k) * pairs + p] = fold_rows(sums[2 * p])
            dots[(2 * k + 1) * pairs + p] = fold_rows(sums[2 * p + 1])

    shift = my_pair * quarter
    half = far_rows // 2

    def sweep_far(body):
        def step(c, carry):
            return body(pl.multiple_of(8 + half * c, 8), half, carry)

        lax.fori_loop(0, 2, step, ())

    def far_pairs(s):
        if not early[s]:
            return
        take(s)
        ids = [far_cells[s, pl.ds(r, 1), :] for r in range(2 * pairs)]
        sweep_far(functools.partial(start_rows, early[s], far_volts.at[s], far_basis.at[s], ids, shift))
        for k in range(STEPS - 1):
            sweep_far(functools.partial(advance, early[s], far_basis.at[s], shift, k))

    n_dots = 2 * STEPS * pairs
    part = jnp.sum(dots[...], axis=1)
    message[...] = jnp.broadcast_to(jnp.sum(part, axis=1, keepdims=True), (n_dots, LANES))

    def reduce_start(axis, me, count, gather, phase):
        copies = []
        for step in range(1, count):
            copies.append(
                pltpu.make_async_remote_copy(
                    src_ref=message,
                    dst_ref=gather.at[me],
                    send_sem=red_send.at[phase, step - 1],
                    recv_sem=red_recv.at[phase, step - 1],
                    device_id={axis: around(me, step, count)},
                    device_id_type=MESH,
                )
            )
        for copy in copies:
            copy.start()
        gather[me] = message[...]
        return copies

    def reduce_end(copies, count, gather):
        for copy in copies:
            copy.wait()
        total = gather[0]
        for i in range(1, count):
            total = total + gather[i]
        return total

    copies = reduce_start("col", my_col, n_col, gather_col, 0)
    message[...] = reduce_end(copies, n_col, gather_col)
    copies = reduce_start("row", my_row, n_row, gather_row, 1)
    far_pairs(0)
    totals = reduce_end(copies, n_row, gather_row)
    parts = solve_coefficients([totals[j * pairs : (j + 1) * pairs] for j in range(2 * STEPS)])
    for k in range(STEPS):
        shares[pl.ds(k * pairs, pairs), :] = parts[k]
    tell = []
    slots = [s for s in range(n_pair - 1) if early[s]]
    for s in slots:
        tell.append(
            pltpu.make_async_remote_copy(
                src_ref=shares,
                dst_ref=far_shares.at[s],
                send_sem=far_send.at[15 + s],
                recv_sem=far_recv.at[15 + s],
                device_id={"pair": owners[s]},
                device_id_type=MESH,
            )
        )
        tell[-1].start()

    def volts_rows(count, field, basis, shares, shift, start, height, carry):
        at = pl.ds(start, height)
        for p in range(count):
            for t in range(wide):
                change = shares[pl.ds(p, 1), :] * basis[0, p, t, at, :]
                for k in range(1, STEPS):
                    change = change + shares[pl.ds(k * pairs + p, 1), :] * basis[k, p, t, at, :]
                value = field[p, t, at, :] + scale[t, pl.ds(pl.multiple_of(start + shift, 8), height), :] * change
                field[p, t, at, :] = value
        return carry

    for copy in moves.values():
        copy.wait_send()
    sweep_border(functools.partial(volts_rows, pairs, volts, basis, shares, 0))
    sweep_own(functools.partial(volts_rows, pairs, volts, basis, shares, 0))
    stores = []
    for t in range(tiles):
        for p in range(pairs):
            stores.append(
                pltpu.make_async_copy(
                    volts.at[p, t, pl.ds(OWN, rows)],
                    volts_out.at[p, :, pl.ds(t * LANES, LANES)],
                    store_sem.at[len(stores)],
                )
            )


    def currents(row, height, fields, store):
        start = pl.multiple_of(OWN + row, 8)
        own_at = pl.ds(start, height)
        right = [link_e[t, own_at, :] for t in range(wide)]
        total, peak = [None] * tiles, [None] * tiles
        for field, first, p in fields:
            at, up_at, down_at = pl.ds(first, height), pl.ds(first - 1, height), pl.ds(first + 1, height)
            here = [field[p, t, at, :] for t in range(wide)]
            there = east(here)
            flow = [jnp.abs(right[t] * (here[t] - there[t])) for t in range(wide)]
            flow_w = west(flow)
            for t in range(tiles):
                value = flow[t] + flow_w[t]
                value = value + jnp.abs(link_n[t, own_at, :] * (here[t] - field[p, t, up_at, :]))
                value = value + jnp.abs(link_n[t, pl.ds(start + 1, height), :] * (here[t] - field[p, t, down_at, :]))
                value = 0.5 * value
                total[t] = value if total[t] is None else total[t] + value
                peak[t] = value if peak[t] is None else jnp.maximum(peak[t], value)
        for t in range(tiles):
            store(pl.ds(t * LANES, LANES), total[t], peak[t])

    q_next, q_prev, q_far = owners
    def span(index, u):
        return pl.ds(pl.multiple_of(index * quarter + u * unit, unit), unit)

    def ring(slot, src, dst, who):
        copy = pltpu.make_async_remote_copy(
            src_ref=src,
            dst_ref=dst,
            send_sem=ring_send.at[slot],
            recv_sem=ring_recv.at[slot],
            device_id={"pair": who},
            device_id_type=MESH,
        )
        copy.start()
        return copy

    sent = {}

    def spread(u, name):
        at = span(my_pair, u)
        if name == "up":
            sent["up", u] = ring(u, result.at[:, at], result.at[:, at], q_next)
        else:
            sent["down", u] = ring(4 + u, result.at[:, at], result.at[:, at], q_prev)

    arrays = late.shape[1]
    near_pairs = range(early[0], pairs)
    in_block = BLOCK // unit
    for i in range(quarter // BLOCK):
        for n, (owner, target) in enumerate(((q_next, late_prev), (q_prev, late_next))):
            row = pl.multiple_of(owner * quarter + BLOCK * i, BLOCK)
            at = pl.ds(BLOCK * i, BLOCK)

            def store(lanes, total, peak, n=n, at=at):
                late[n, 0, at, lanes] = total
                if arrays > 1:
                    late[n, 1, at, lanes] = peak

            currents(row, BLOCK, [(volts, pl.multiple_of(OWN + row, 8), p) for p in near_pairs], store)
            for u in range(i * in_block, (i + 1) * in_block):
                part = pl.ds(u * unit, unit)
                sent["late", n, u] = ring(12 + 2 * u + n, late.at[n, :, part], target.at[:, part], owner)
    for store in stores:
        store.start()

    far_pairs(1)
    far_pairs(2)
    for s, told in zip(slots, tell):
        told.wait_recv()
        sweep_far(functools.partial(volts_rows, early[s], far_volts.at[s], far_basis.at[s], far_shares.at[s], shift))
    for i in range(quarter // BLOCK):

        def own_block(h, carry, i=i):
            at = BLOCK * i + HALF_BLOCK * h
            row = pl.multiple_of(my_pair * quarter + at, HALF_BLOCK)
            fields = [(volts, pl.multiple_of(OWN + row, 8), p) for p in range(pairs)]
            for s in range(n_pair - 1):
                fields += [(far_volts.at[s], pl.multiple_of(OWN + at, 8), p) for p in range(early[s])]

            def store(lanes, total, peak):
                result[0, pl.ds(row, HALF_BLOCK), lanes] = total
                result[1, pl.ds(row, HALF_BLOCK), lanes] = peak

            currents(row, HALF_BLOCK, fields, store)
            return carry

        lax.fori_loop(0, BLOCK // HALF_BLOCK, own_block, 0)
        for u in range(i * in_block, (i + 1) * in_block):
            at, rows_of = span(my_pair, u), pl.ds(u * unit, unit)
            sent["late", 0, u].wait_recv()
            sent["late", 1, u].wait_recv()
            result[0, at, :] = result[0, at, :] + late_prev[0, rows_of, :] + late_next[0, rows_of, :]
            result[1, at, :] = jnp.maximum(
                result[1, at, :], jnp.maximum(late_prev[arrays - 1, rows_of, :], late_next[arrays - 1, rows_of, :])
            )
            spread(u, "up")
            spread(u, "down")

    def keep(index, slot, first, count):
        at = pl.ds(pl.multiple_of(index * quarter + first * unit, unit), count * unit)
        stores.append(pltpu.make_async_copy(result.at[:, at], result_out.at[:, at], store_sem.at[pairs * tiles + slot]))
        stores[-1].start()

    for i in range(2):
        sent["up", i].wait_recv()
        at = span(q_prev, i)
        sent["over", i] = ring(8 + i, result.at[:, at], result.at[:, at], q_next)
        sent["down", 2 + i].wait_recv()
        at = span(q_next, 2 + i)
        sent["over", 2 + i] = ring(10 + i, result.at[:, at], result.at[:, at], q_prev)
    keep(my_pair, 0, 0, 4)
    for i in range(2):
        sent["up", 2 + i].wait_recv()
        sent["down", i].wait_recv()
    keep(q_prev, 1, 0, 4)
    keep(q_next, 2, 0, 4)
    for i in range(2):
        sent["over", i].wait_recv()
        sent["over", 2 + i].wait_recv()
        keep(q_far, 3 + 2 * i, i, 1)
        keep(q_far, 4 + 2 * i, 2 + i, 1)
    for copy in sent.values():
        copy.wait_send()
    for copy in tell:
        copy.wait_send()
    for store in stores:
        store.wait()


def write_out(volts, result, volts_out, sum_out, max_out, held_volts, held_result, load_sem, store_sem):
    pairs, rows = volts.shape[:2]
    part = rows // PIECES
    loads, stores = [], []
    for i in range(PIECES):
        at = pl.ds(i * part, part)
        moves = [(volts.at[p, at], held_volts.at[p, at], volts_out.at[p, at]) for p in range(pairs)]
        moves.append((result.at[0, at], held_result.at[0, at], sum_out.at[at]))
        moves.append((result.at[1, at], held_result.at[1, at], max_out.at[at]))
        for src, held, dst in moves:
            n = len(loads)
            loads.append(pltpu.make_async_copy(src, held, load_sem.at[n]))
            stores.append(pltpu.make_async_copy(held, dst, store_sem.at[n]))
    for load in loads:
        load.start()
    for load, store in zip(loads, stores):
        load.wait()
        store.start()
    for store in stores:
        store.wait()


def on_device(mesh_sizes, conductance, valid_mask, focal_cells, initial_volts):
    rows, columns = conductance.shape
    pairs = initial_volts.shape[0]
    tiles = columns // LANES
    n_pair, n_row, n_col = mesh_sizes
    sizes = (pairs, rows, tiles, n_pair, n_row, n_col)
    wide, tall, fold, quarter = tiles + 1, rows + 32, rows // 4, rows // 4
    n_dots = 2 * STEPS * pairs
    others = n_pair - 1
    arrays = min(2, pairs - NEAR_EARLY)
    pack_rows = 8 * ((quarter // 8 + 2 + 3) // 4)
    f32 = jnp.float32
    stay = pl.BlockSpec(memory_space=pltpu.HBM)
    raster = pltpu.VMEM((wide, tall, LANES), f32)
    volts, result = pl.pallas_call(
        functools.partial(kernel, sizes),
        out_shape=(
            jax.ShapeDtypeStruct((pairs, rows, columns), f32),
            jax.ShapeDtypeStruct((2, rows, columns), f32),
        ),
        in_specs=[stay, stay, pl.BlockSpec(memory_space=pltpu.SMEM), stay],
        out_specs=(stay, stay),
        scratch_shapes=[
            pltpu.VMEM((tiles, rows, LANES), f32),
            pltpu.VMEM((tiles, rows, LANES), jnp.int32),
            pltpu.VMEM((pairs, wide, tall, LANES), f32),
            raster,
            raster,
            raster,
            raster,
            raster,
            raster,
            raster,
            pltpu.VMEM((STEPS, pairs, wide, tall, LANES), f32),
            pltpu.VMEM((fold, LANES), f32),
            pltpu.VMEM((fold, LANES), f32),
            pltpu.VMEM((fold + 16, LANES), f32),
            pltpu.VMEM((fold + 16, LANES), f32),
            pltpu.VMEM((n_dots, 8, LANES), f32),
            pltpu.VMEM((n_dots, LANES), f32),
            pltpu.VMEM((n_col, n_dots, LANES), f32),
            pltpu.VMEM((n_row, n_dots, LANES), f32),
            pltpu.VMEM((2, rows, columns), f32),
            pltpu.VMEM((2, arrays, quarter, columns), f32),
            pltpu.VMEM((arrays, quarter, columns), f32),
            pltpu.VMEM((arrays, quarter, columns), f32),
            pltpu.VMEM((others, pairs, wide, quarter + 32, LANES), f32),
            pltpu.VMEM((others, STEPS, pairs, wide, quarter + 32, LANES), f32),
            pltpu.VMEM((others, pack_rows, LANES), f32),
            pltpu.VMEM((others, pack_rows, LANES), f32),
            pltpu.VMEM((8, LANES), jnp.int32),
            pltpu.VMEM((others, 8, LANES), jnp.int32),
            pltpu.VMEM((8 * ((STEPS * pairs + 7) // 8), LANES), f32),
            pltpu.VMEM((others, 8 * ((STEPS * pairs + 7) // 8), LANES), f32),
            pltpu.SemaphoreType.DMA(((2 + pairs) * tiles,)),
            pltpu.SemaphoreType.DMA((pairs * tiles + 7,)),
            pltpu.SemaphoreType.DMA((10,)),
            pltpu.SemaphoreType.DMA((10,)),
            pltpu.SemaphoreType.DMA((2, max(n_col, n_row) - 1)),
            pltpu.SemaphoreType.DMA((2, max(n_col, n_row) - 1)),
            pltpu.SemaphoreType.DMA((18,)),
            pltpu.SemaphoreType.DMA((18,)),
            pltpu.SemaphoreType.DMA((20,)),
            pltpu.SemaphoreType.DMA((20,)),
        ],
        compiler_params=pltpu.CompilerParams(
            collective_id=0, has_side_effects=True, vmem_limit_bytes=int(61 * 1024 * 1024)
        ),
    )(conductance, valid_mask, focal_cells, initial_volts)
    flat = jax.ShapeDtypeStruct((rows, columns), f32)
    return pl.pallas_call(
        write_out,
        out_shape=(jax.ShapeDtypeStruct((pairs, rows, columns), f32), flat, flat),
        in_specs=[stay, stay],
        out_specs=(stay, stay, stay),
        scratch_shapes=[
            pltpu.VMEM((pairs, rows, columns), f32),
            pltpu.VMEM((2, rows, columns), f32),
            pltpu.SemaphoreType.DMA((PIECES * (pairs + 2),)),
            pltpu.SemaphoreType.DMA((PIECES * (pairs + 2),)),
        ],
    )(volts, result)


def solution(mesh):
    in_specs = (P("row", "col"), P("row", "col"), P("pair", None), P("pair", "row", "col"))
    out_specs = (P("pair", "row", "col"), P("row", "col"), P("row", "col"))
    sizes = (mesh.shape["pair"], mesh.shape["row"], mesh.shape["col"])
    return jax.shard_map(
        functools.partial(on_device, sizes), mesh=mesh, in_specs=in_specs, out_specs=out_specs, check_vma=False
    )
```

```python
import functools

import jax
import jax.numpy as jnp
from jax import lax
from jax.experimental import pallas as pl
from jax.experimental.pallas import tpu as pltpu
from jax.sharding import PartitionSpec as P

MESH = pl.DeviceIdType.MESH
LEAKAGE = 0.01
STEPS = 6
LANES = 128
EDGE = 8
OWN = 16
BLOCK = 32
SWEEP = 64
HALF_BLOCK = 16
NEAR_EARLY = 1
PIECES = 2


def lane_ids(height):
    return lax.broadcasted_iota(jnp.int32, (height, LANES), 1)


def east(tiles):
    last = lane_ids(tiles[0].shape[0]) == LANES - 1
    rolled = [pltpu.roll(tile, LANES - 1, 1) for tile in tiles]
    return [jnp.where(last, rolled[(t + 1) % len(tiles)], rolled[t]) for t in range(len(tiles))]


def west(tiles):
    first = lane_ids(tiles[0].shape[0]) == 0
    rolled = [pltpu.roll(tile, 1, 1) for tile in tiles]
    return [jnp.where(first, rolled[t - 1], rolled[t]) for t in range(len(tiles))]


def link(a, b):
    return jnp.where(jnp.minimum(a, b) > 0.0, 0.5 * (a + b), 0.0)


def solve_coefficients(totals):
    same = [totals[2 * k] for k in range(STEPS)]
    after = [totals[2 * k + 1] for k in range(STEPS)]
    nu = [same[1], after[1]]
    for k in range(1, STEPS - 1):
        nu.append(2.0 * same[k + 1] - nu[0])
        nu.append(2.0 * after[k + 1] - nu[1])
    rho = [same[0], after[0], nu[0]]
    for k in range(1, STEPS - 2):
        rho.append(2.0 * nu[k] - rho[k])
    gram = [[None] * STEPS for _ in range(STEPS)]
    gram[0][0] = rho[0] - rho[1]
    for j in range(1, STEPS):
        gram[0][j] = rho[j] - nu[j - 1]
    for i in range(STEPS - 1):
        for j in range(i, STEPS - 1):
            before = abs(j - 1)
            gram[i + 1][j + 1] = 0.5 * (nu[i + j] + nu[abs(i - j)]) - 0.25 * (
                nu[i + j + 1] + nu[abs(i - j - 1)] + nu[i + before] + nu[abs(i - before)]
            )
    right = list(rho)
    least = [3e-7 * gram[j][j] for j in range(STEPS)]
    inverse, factors = [], {}
    for j in range(STEPS):
        pivot = gram[j][j]
        usable = pivot > least[j]
        inverse.append(jnp.where(usable, 1.0 / jnp.where(usable, pivot, 1.0), 0.0))
        for i in range(j + 1, STEPS):
            factors[i, j] = gram[j][i] * inverse[j]
        for i in range(j + 1, STEPS):
            for m in range(i, STEPS):
                gram[i][m] = gram[i][m] - factors[i, j] * gram[j][m]
            right[i] = right[i] - factors[i, j] * right[j]
    out = [right[j] * inverse[j] for j in range(STEPS)]
    for i in reversed(range(STEPS)):
        for j in range(i + 1, STEPS):
            out[i] = out[i] - factors[j, i] * out[j]
    return out


def kernel(
    sizes,
    cond_in,
    mask_in,
    focal,
    volts_in,
    volts_out,
    result_out,
    stage_cond,
    stage_mask,
    volts,
    cond,
    link_e,
    link_n,
    scale,
    coef_c,
    coef_e,
    coef_n,
    basis,
    pack_e,
    pack_w,
    land_w,
    land_e,
    dots,
    message,
    gather_col,
    gather_row,
    result,
    late,
    late_prev,
    late_next,
    far_volts,
    far_basis,
    far_pack,
    land_pack,
    cells,
    far_cells,
    shares,
    far_shares,
    load_sem,
    store_sem,
    halo_send,
    halo_recv,
    red_send,
    red_recv,
    far_send,
    far_recv,
    ring_send,
    ring_recv,
):
    pairs, rows, tiles, n_pair, n_row, n_col = sizes
    wide = tiles + 1
    chunks = rows // 8
    fold = rows // 4
    fold_chunks = fold // 8
    quarter = rows // 4
    unit = quarter // 4
    my_pair, my_row, my_col = lax.axis_index("pair"), lax.axis_index("row"), lax.axis_index("col")

    def around(index, step, count):
        return lax.rem(index + (step + count), count)

    loads = []
    for t in range(tiles):
        lanes = pl.ds(t * LANES, LANES)
        loads.append(pltpu.make_async_copy(cond_in.at[:, lanes], stage_cond.at[t], load_sem.at[len(loads)]))
        loads.append(pltpu.make_async_copy(mask_in.at[:, lanes], stage_mask.at[t], load_sem.at[len(loads)]))
        for p in range(pairs):
            loads.append(
                pltpu.make_async_copy(
                    volts_in.at[p, :, lanes], volts.at[p, t, pl.ds(OWN, rows)], load_sem.at[len(loads)]
                )
            )
    for load in loads:
        load.start()

    north, south = around(my_row, -1, n_row), around(my_row, 1, n_row)
    westward, eastward = around(my_col, -1, n_col), around(my_col, 1, n_col)
    partners = [{"col": around(my_col, step, n_col)} for step in range(1, n_col)]
    partners += [{"row": around(my_row, step, n_row)} for step in range(1, n_row)]
    partners += [{"row": r, "col": c} for r in (north, south) for c in (westward, eastward)]
    partners += [{"pair": around(my_pair, step, n_pair)} for step in range(1, n_pair)]
    barrier = pltpu.get_barrier_semaphore()
    for partner in partners:
        pl.semaphore_signal(barrier, inc=1, device_id=partner, device_id_type=MESH)

    zero = jnp.zeros((8, LANES), jnp.float32)
    for start in (0, rows + 3 * 8):
        at = pl.ds(start, 8)
        for t in range(wide):
            for ref in (cond, scale, link_n, coef_n):
                ref[t, at, :] = zero
            for p in range(pairs):
                volts[p, t, at, :] = zero
                for k in range(STEPS):
                    basis[k, p, t, at, :] = zero
    for start in (0, quarter + 3 * 8):
        at = pl.ds(start, 8)
        for s in range(n_pair - 1):
            for p in range(pairs):
                for t in range(wide):
                    far_volts[s, p, t, at, :] = zero
                    for k in range(STEPS):
                        far_basis[s, k, p, t, at, :] = zero
    row_of = lax.broadcasted_iota(jnp.int32, (8, LANES), 0)
    packed_cells = jnp.zeros((8, LANES), jnp.int32)
    for p in range(pairs):
        for j in range(2):
            packed_cells = jnp.where(row_of == 2 * p + j, focal[p, j], packed_cells)
    cells[...] = packed_cells

    for load in loads:
        load.wait()

    def own_cond(c, carry):
        at = pl.ds(pl.multiple_of(8 * c, 8), 8)
        to = pl.ds(pl.multiple_of(OWN + 8 * c, 8), 8)
        for t in range(tiles):
            cond[t, to, :] = stage_cond[t, at, :] * stage_mask[t, at, :].astype(jnp.float32)
        return carry

    lax.fori_loop(0, chunks, own_cond, 0)

    lane = lane_ids(8)

    def pack(c, carry):
        for side, tile, ref in ((0, 0, pack_w), (1, tiles - 1, pack_e)):
            packed = jnp.zeros((8, LANES), jnp.float32)
            for g in range(4):
                at = pl.ds(pl.multiple_of(OWN + g * fold + 8 * c, 8), 8)
                fields = [volts[p, tile, at, :] for p in range(pairs)] + [cond[tile, at, :]]
                for f, value in enumerate(fields):
                    low = 32 * g + 8 * f
                    first = 0 if side == 0 else LANES - 8
                    shift = (low - first) % LANES
                    moved = pltpu.roll(value, shift, 1) if shift else value
                    packed = jnp.where((lane >= low) & (lane < low + 8), moved, packed)
            ref[pl.ds(pl.multiple_of(8 * c, 8), 8), :] = packed
        return carry

    lax.fori_loop(0, fold_chunks, pack, 0)
    pl.semaphore_wait(barrier, len(partners))

    top, bottom = pl.ds(OWN, 8), pl.ds(OWN + rows - 8, 8)
    over, under = pl.ds(OWN - 8, 8), pl.ds(OWN + rows, 8)
    mid = pl.ds(8, fold)
    halo = [
        (volts.at[:, pl.ds(0, tiles), top], volts.at[:, pl.ds(0, tiles), under], {"row": north}),
        (cond.at[pl.ds(0, tiles), top], cond.at[pl.ds(0, tiles), under], {"row": north}),
        (volts.at[:, pl.ds(0, tiles), bottom], volts.at[:, pl.ds(0, tiles), over], {"row": south}),
        (cond.at[pl.ds(0, tiles), bottom], cond.at[pl.ds(0, tiles), over], {"row": south}),
        (pack_w, land_e.at[mid], {"col": westward}),
        (pack_e, land_w.at[mid], {"col": eastward}),
        (pack_w.at[pl.ds(0, 8)], land_e.at[pl.ds(fold + 8, 8)], {"row": north, "col": westward}),
        (pack_w.at[pl.ds(fold - 8, 8)], land_e.at[pl.ds(0, 8)], {"row": south, "col": westward}),
        (pack_e.at[pl.ds(0, 8)], land_w.at[pl.ds(fold + 8, 8)], {"row": north, "col": eastward}),
        (pack_e.at[pl.ds(fold - 8, 8)], land_w.at[pl.ds(0, 8)], {"row": south, "col": eastward}),
    ]
    halo = [
        pltpu.make_async_remote_copy(
            src_ref=src,
            dst_ref=dst,
            send_sem=halo_send.at[i],
            recv_sem=halo_recv.at[i],
            device_id=who,
            device_id_type=MESH,
        )
        for i, (src, dst, who) in enumerate(halo)
    ]
    for copy in halo:
        copy.start()

    ahead = (1, n_pair - 1, 2)
    owners = [around(my_pair, step, n_pair) for step in ahead]
    early = (min(NEAR_EARLY, pairs), min(NEAR_EARLY, pairs), pairs)
    moves = {}

    def give(s, kind, src, dst):
        slot = 5 * s + len([key for key in moves if key[0] == s])
        moves[s, kind] = pltpu.make_async_remote_copy(
            src_ref=src,
            dst_ref=dst,
            send_sem=far_send.at[slot],
            recv_sem=far_recv.at[slot],
            device_id={"pair": owners[s]},
            device_id_type=MESH,
        )
        moves[s, kind].start()

    def give_main(s):
        if not early[s]:
            return
        start = pl.multiple_of(OWN + owners[s] * quarter, 8)
        give(
            s,
            "main",
            volts.at[pl.ds(0, early[s]), pl.ds(0, tiles), pl.ds(start, quarter)],
            far_volts.at[s, pl.ds(0, early[s]), pl.ds(0, tiles), pl.ds(OWN, quarter)],
        )

    def give_border(s):
        if not early[s]:
            return
        start = OWN + owners[s] * quarter
        for kind, offset in (("over", -EDGE), ("under", quarter)):
            give(
                s,
                kind,
                volts.at[pl.ds(0, early[s]), pl.ds(0, tiles), pl.ds(pl.multiple_of(start + offset, 8), EDGE)],
                far_volts.at[s, pl.ds(0, early[s]), pl.ds(0, tiles), pl.ds(OWN + offset, EDGE)],
            )
        give(s, "pack", far_pack.at[s], land_pack.at[s])
        give(s, "cells", cells, far_cells.at[s])

    give_main(0)
    give_main(1)
    give_main(2)
    for copy in halo:
        copy.wait()

    has_n = (my_row > 0).astype(jnp.float32)
    has_s = (my_row < n_row - 1).astype(jnp.float32)
    has_w = (my_col > 0).astype(jnp.float32)
    has_e = (my_col < n_col - 1).astype(jnp.float32)
    for t in range(tiles):
        cond[t, over, :] = cond[t, over, :] * has_n
        cond[t, under, :] = cond[t, under, :] * has_s

    def unpack(source, g, to, keep):
        left = land_w[source, :]
        right = land_e[source, :]
        for f in range(pairs + 1):
            low = 32 * g + 8 * f
            a = pltpu.roll(left, (LANES - 8 - low) % LANES, 1)
            b = pltpu.roll(right, (LANES - low) % LANES, 1) if low else right
            if f == pairs:
                a, b = a * (has_w * keep), b * (has_e * keep)
            value = jnp.where(lane < 8, b, jnp.where(lane >= LANES - 8, a, 0.0))
            if f == pairs:
                cond[tiles, to, :] = value
            else:
                volts[f, tiles, to, :] = value

    def unpack_chunk(c, carry):
        for g in range(4):
            unpack(
                pl.ds(pl.multiple_of(8 + 8 * c, 8), 8),
                g,
                pl.ds(pl.multiple_of(OWN + g * fold + 8 * c, 8), 8),
                1.0,
            )
        return carry

    lax.fori_loop(0, fold_chunks, unpack_chunk, 0)
    unpack(pl.ds(0, 8), 3, over, has_n)
    unpack(pl.ds(fold + 8, 8), 0, under, has_s)

    far_rows = quarter + 2 * EDGE

    def pack_place(j, p):
        return 32 * (j % 4) + 16 * p

    for s in range(n_pair - 1):
        start = OWN - EDGE + owners[s] * quarter
        for c in range(far_pack.shape[1] // 8):
            packed = jnp.zeros((8, LANES), jnp.float32)
            for j in range(4 * c, min(4 * c + 4, far_rows // 8)):
                for p in range(early[s]):
                    low = pack_place(j, p)
                    value = volts[p, tiles, pl.ds(pl.multiple_of(start + 8 * j, 8), 8), :]
                    moved = pltpu.roll(value, (low + 8) % LANES, 1)
                    packed = jnp.where((lane >= low) & (lane < low + 16), moved, packed)
            far_pack[s, pl.ds(8 * c, 8), :] = packed
    give_border(0)
    give_border(1)
    give_border(2)

    def take(s):
        for kind in ("main", "over", "under", "pack", "cells"):
            moves[s, kind].wait_recv()
        for j in range(far_rows // 8):
            for p in range(early[s]):
                moved = pltpu.roll(
                    land_pack[s, pl.ds(8 * (j // 4), 8), :], (2 * LANES - 8 - pack_place(j, p)) % LANES, 1
                )
                far_volts[s, p, tiles, pl.ds(8 + 8 * j, 8), :] = jnp.where(
                    (lane < 8) | (lane >= LANES - 8), moved, 0.0
                )

    def sweep_own(body, carry=(), height=SWEEP):
        def step(c, carry):
            return body(pl.multiple_of(OWN + height * c, 8), height, carry)

        return lax.fori_loop(0, rows // height, step, carry)

    def sweep_border(body):
        def step(i, carry):
            return body(pl.multiple_of(OWN - 8 + i * (rows + 8), 8), 8, carry)

        lax.fori_loop(0, 2, step, ())

    def links_rows(start, height, carry):
        at = pl.ds(start, height)
        here = [cond[t, at, :] for t in range(wide)]
        right = [link(a, b) for a, b in zip(here, east(here))]
        left = west(right)
        for t in range(wide):
            up = link(here[t], cond[t, pl.ds(start - 1, height), :])
            down = link(here[t], cond[t, pl.ds(start + 1, height), :])
            diagonal = up + down + left[t] + right[t] + LEAKAGE * here[t] + jnp.where(here[t] > 0.0, 0.0, 1.0)
            most = jnp.maximum(diagonal, 1.0)
            root = lax.rsqrt(most)
            root = root * (1.5 - 0.5 * most * root * root)
            link_e[t, at, :] = right[t]
            link_n[t, at, :] = up
            scale[t, at, :] = root
            coef_c[t, at, :] = 2.0 * jnp.maximum(1.0 - diagonal, 0.0)
        return carry

    sweep_border(links_rows)
    sweep_own(links_rows)

    width_all = tiles * LANES * n_col

    def coefficient_rows(start, height, carry):
        at = pl.ds(start, height)
        root = [scale[t, at, :] for t in range(wide)]
        root_e = east(root)
        for t in range(wide):
            coef_e[t, at, :] = 2.0 * link_e[t, at, :] * root[t] * root_e[t]
            coef_n[t, at, :] = 2.0 * link_n[t, at, :] * root[t] * scale[t, pl.ds(start - 1, height), :]
        return carry

    def start_rows(count, field, out, ids, shift, start, height, carry):
        at, up_at, down_at = pl.ds(start, height), pl.ds(start - 1, height), pl.ds(start + 1, height)
        base = pl.multiple_of(start + shift, 8)
        own_at = pl.ds(base, height)
        column = lane_ids(height)
        sub = lax.broadcasted_iota(jnp.int32, (height, LANES), 0)
        first = my_col * (tiles * LANES)
        columns = [first + t * LANES + column for t in range(tiles)]
        columns.append(first + jnp.where(column < 64, tiles * LANES, -LANES) + column)
        right = [link_e[t, own_at, :] for t in range(wide)]
        flat = (my_row * rows + base - OWN + sub) * width_all
        own = []
        for t in range(wide):
            value = cond[t, own_at, :]
            own.append(LEAKAGE * value + jnp.where(value > 0.0, 0.0, 1.0))
        for p in range(count):
            here = [field[p, t, at, :] for t in range(wide)]
            there = east(here)
            flow = [right[t] * (here[t] - there[t]) for t in range(wide)]
            flow_w = west(flow)
            for t in range(wide):
                total = flow[t] - flow_w[t] + own[t] * here[t]
                total = total + link_n[t, own_at, :] * (here[t] - field[p, t, up_at, :])
                total = total + link_n[t, pl.ds(base + 1, height), :] * (here[t] - field[p, t, down_at, :])
                cell = flat + columns[t]
                inject = jnp.where(cell == ids[2 * p], 1.0, 0.0) - jnp.where(cell == ids[2 * p + 1], 1.0, 0.0)
                out[0, p, t, at, :] = scale[t, own_at, :] * (inject - total)
        return carry

    sweep_border(coefficient_rows)
    sweep_own(coefficient_rows)
    start_own = functools.partial(
        start_rows, pairs, volts, basis, [focal[p, j] for p in range(pairs) for j in range(2)], 0
    )
    sweep_border(start_own)
    sweep_own(start_own)

    def advance(fields, basis, shift, k, start, height, sums):
        at, up_at, down_at = pl.ds(start, height), pl.ds(start - 1, height), pl.ds(start + 1, height)
        base = pl.multiple_of(start + shift, 8)
        own_at = pl.ds(base, height)
        final = k == STEPS - 1
        count = tiles if final else wide
        right = [coef_e[t, own_at, :] for t in range(wide)]
        out = []
        for p in range(fields):
            here = [basis[k, p, t, at, :] for t in range(wide)]
            there = east(here)
            back = west([right[t] * here[t] for t in range(wide)])
            same = jnp.zeros((height, LANES), jnp.float32)
            step = jnp.zeros((height, LANES), jnp.float32)
            for t in range(count):
                value = coef_c[t, own_at, :] * here[t] + right[t] * there[t] + back[t]
                value = value + coef_n[t, own_at, :] * basis[k, p, t, up_at, :]
                value = value + coef_n[t, pl.ds(base + 1, height), :] * basis[k, p, t, down_at, :]
                value = 0.5 * value if k < 2 else value - basis[k - 1, p, t, at, :]
                if not final:
                    basis[k + 1, p, t, at, :] = value
                if sums and t < tiles:
                    same = same + here[t] * here[t]
                    step = step + here[t] * value
            if sums:
                out += [sums[2 * p] + same, sums[2 * p + 1] + step]
        return tuple(out) if sums else sums

    def fold_rows(value):
        total = value[:8]
        for i in range(1, SWEEP // 8):
            total = total + value[8 * i : 8 * i + 8]
        return total

    for k in range(STEPS):
        if k < STEPS - 1:
            sweep_border(functools.partial(advance, pairs, basis, 0, k))
        tall_zero = jnp.zeros((SWEEP, LANES), jnp.float32)
        sums = sweep_own(functools.partial(advance, pairs, basis, 0, k), (tall_zero,) * (2 * pairs), SWEEP)
        for p in range(pairs):
            dots[(2 * k) * pairs + p] = fold_rows(sums[2 * p])
            dots[(2 * k + 1) * pairs + p] = fold_rows(sums[2 * p + 1])

    shift = my_pair * quarter
    half = far_rows // 2

    def sweep_far(body):
        def step(c, carry):
            return body(pl.multiple_of(8 + half * c, 8), half, carry)

        lax.fori_loop(0, 2, step, ())

    def far_pairs(s):
        if not early[s]:
            return
        take(s)
        ids = [far_cells[s, pl.ds(r, 1), :] for r in range(2 * pairs)]
        sweep_far(functools.partial(start_rows, early[s], far_volts.at[s], far_basis.at[s], ids, shift))
        for k in range(STEPS - 1):
            sweep_far(functools.partial(advance, early[s], far_basis.at[s], shift, k))

    n_dots = 2 * STEPS * pairs
    part = jnp.sum(dots[...], axis=1)
    message[...] = jnp.broadcast_to(jnp.sum(part, axis=1, keepdims=True), (n_dots, LANES))

    def reduce_start(axis, me, count, gather, phase):
        copies = []
        for step in range(1, count):
            copies.append(
                pltpu.make_async_remote_copy(
                    src_ref=message,
                    dst_ref=gather.at[me],
                    send_sem=red_send.at[phase, step - 1],
                    recv_sem=red_recv.at[phase, step - 1],
                    device_id={axis: around(me, step, count)},
                    device_id_type=MESH,
                )
            )
        for copy in copies:
            copy.start()
        gather[me] = message[...]
        return copies

    def reduce_end(copies, count, gather):
        for copy in copies:
            copy.wait()
        total = gather[0]
        for i in range(1, count):
            total = total + gather[i]
        return total

    copies = reduce_start("col", my_col, n_col, gather_col, 0)
    message[...] = reduce_end(copies, n_col, gather_col)
    copies = reduce_start("row", my_row, n_row, gather_row, 1)
    far_pairs(0)
    totals = reduce_end(copies, n_row, gather_row)
    parts = solve_coefficients([totals[j * pairs : (j + 1) * pairs] for j in range(2 * STEPS)])
    for k in range(STEPS):
        shares[pl.ds(k * pairs, pairs), :] = parts[k]
    tell = []
    slots = [s for s in range(n_pair - 1) if early[s]]
    for s in slots:
        tell.append(
            pltpu.make_async_remote_copy(
                src_ref=shares,
                dst_ref=far_shares.at[s],
                send_sem=far_send.at[15 + s],
                recv_sem=far_recv.at[15 + s],
                device_id={"pair": owners[s]},
                device_id_type=MESH,
            )
        )
        tell[-1].start()

    def volts_rows(count, field, basis, shares, shift, start, height, carry):
        at = pl.ds(start, height)
        for p in range(count):
            for t in range(wide):
                change = shares[pl.ds(p, 1), :] * basis[0, p, t, at, :]
                for k in range(1, STEPS):
                    change = change + shares[pl.ds(k * pairs + p, 1), :] * basis[k, p, t, at, :]
                value = field[p, t, at, :] + scale[t, pl.ds(pl.multiple_of(start + shift, 8), height), :] * change
                field[p, t, at, :] = value
        return carry

    for copy in moves.values():
        copy.wait_send()
    sweep_border(functools.partial(volts_rows, pairs, volts, basis, shares, 0))
    sweep_own(functools.partial(volts_rows, pairs, volts, basis, shares, 0))
    stores = []
    for t in range(tiles):
        for p in range(pairs):
            stores.append(
                pltpu.make_async_copy(
                    volts.at[p, t, pl.ds(OWN, rows)],
                    volts_out.at[p, :, pl.ds(t * LANES, LANES)],
                    store_sem.at[len(stores)],
                )
            )


    def currents(row, height, fields, store):
        start = pl.multiple_of(OWN + row, 8)
        own_at = pl.ds(start, height)
        right = [link_e[t, own_at, :] for t in range(wide)]
        total, peak = [None] * tiles, [None] * tiles
        for field, first, p in fields:
            at, up_at, down_at = pl.ds(first, height), pl.ds(first - 1, height), pl.ds(first + 1, height)
            here = [field[p, t, at, :] for t in range(wide)]
            there = east(here)
            flow = [jnp.abs(right[t] * (here[t] - there[t])) for t in range(wide)]
            flow_w = west(flow)
            for t in range(tiles):
                value = flow[t] + flow_w[t]
                value = value + jnp.abs(link_n[t, own_at, :] * (here[t] - field[p, t, up_at, :]))
                value = value + jnp.abs(link_n[t, pl.ds(start + 1, height), :] * (here[t] - field[p, t, down_at, :]))
                value = 0.5 * value
                total[t] = value if total[t] is None else total[t] + value
                peak[t] = value if peak[t] is None else jnp.maximum(peak[t], value)
        for t in range(tiles):
            store(pl.ds(t * LANES, LANES), total[t], peak[t])

    q_next, q_prev, q_far = owners
    def span(index, u):
        return pl.ds(pl.multiple_of(index * quarter + u * unit, unit), unit)

    def ring(slot, src, dst, who):
        copy = pltpu.make_async_remote_copy(
            src_ref=src,
            dst_ref=dst,
            send_sem=ring_send.at[slot],
            recv_sem=ring_recv.at[slot],
            device_id={"pair": who},
            device_id_type=MESH,
        )
        copy.start()
        return copy

    sent = {}

    def spread(u, name):
        at = span(my_pair, u)
        if name == "up":
            sent["up", u] = ring(u, result.at[:, at], result.at[:, at], q_next)
        else:
            sent["down", u] = ring(4 + u, result.at[:, at], result.at[:, at], q_prev)

    arrays = late.shape[1]
    near_pairs = range(early[0], pairs)
    in_block = BLOCK // unit
    for i in range(quarter // BLOCK):
        for n, (owner, target) in enumerate(((q_next, late_prev), (q_prev, late_next))):
            row = pl.multiple_of(owner * quarter + BLOCK * i, BLOCK)
            at = pl.ds(BLOCK * i, BLOCK)

            def store(lanes, total, peak, n=n, at=at):
                late[n, 0, at, lanes] = total
                if arrays > 1:
                    late[n, 1, at, lanes] = peak

            currents(row, BLOCK, [(volts, pl.multiple_of(OWN + row, 8), p) for p in near_pairs], store)
            for u in range(i * in_block, (i + 1) * in_block):
                part = pl.ds(u * unit, unit)
                sent["late", n, u] = ring(12 + 2 * u + n, late.at[n, :, part], target.at[:, part], owner)
    for store in stores:
        store.start()

    far_pairs(1)
    far_pairs(2)
    for s, told in zip(slots, tell):
        told.wait_recv()
        sweep_far(functools.partial(volts_rows, early[s], far_volts.at[s], far_basis.at[s], far_shares.at[s], shift))
    for i in range(quarter // BLOCK):

        def own_block(h, carry, i=i):
            at = BLOCK * i + HALF_BLOCK * h
            row = pl.multiple_of(my_pair * quarter + at, HALF_BLOCK)
            fields = [(volts, pl.multiple_of(OWN + row, 8), p) for p in range(pairs)]
            for s in range(n_pair - 1):
                fields += [(far_volts.at[s], pl.multiple_of(OWN + at, 8), p) for p in range(early[s])]

            def store(lanes, total, peak):
                result[0, pl.ds(row, HALF_BLOCK), lanes] = total
                result[1, pl.ds(row, HALF_BLOCK), lanes] = peak

            currents(row, HALF_BLOCK, fields, store)
            return carry

        lax.fori_loop(0, BLOCK // HALF_BLOCK, own_block, 0)
        for u in range(i * in_block, (i + 1) * in_block):
            at, rows_of = span(my_pair, u), pl.ds(u * unit, unit)
            sent["late", 0, u].wait_recv()
            sent["late", 1, u].wait_recv()
            result[0, at, :] = result[0, at, :] + late_prev[0, rows_of, :] + late_next[0, rows_of, :]
            result[1, at, :] = jnp.maximum(
                result[1, at, :], jnp.maximum(late_prev[arrays - 1, rows_of, :], late_next[arrays - 1, rows_of, :])
            )
            spread(u, "up")
            spread(u, "down")

    def keep(index, slot, first, count):
        at = pl.ds(pl.multiple_of(index * quarter + first * unit, unit), count * unit)
        stores.append(pltpu.make_async_copy(result.at[:, at], result_out.at[:, at], store_sem.at[pairs * tiles + slot]))
        stores[-1].start()

    for i in range(2):
        sent["up", i].wait_recv()
        at = span(q_prev, i)
        sent["over", i] = ring(8 + i, result.at[:, at], result.at[:, at], q_next)
        sent["down", 2 + i].wait_recv()
        at = span(q_next, 2 + i)
        sent["over", 2 + i] = ring(10 + i, result.at[:, at], result.at[:, at], q_prev)
    keep(my_pair, 0, 0, 4)
    for i in range(2):
        sent["up", 2 + i].wait_recv()
        sent["down", i].wait_recv()
    keep(q_prev, 1, 0, 4)
    keep(q_next, 2, 0, 4)
    for i in range(2):
        sent["over", i].wait_recv()
        sent["over", 2 + i].wait_recv()
        keep(q_far, 3 + 2 * i, i, 1)
        keep(q_far, 4 + 2 * i, 2 + i, 1)
    for copy in sent.values():
        copy.wait_send()
    for copy in tell:
        copy.wait_send()
    for store in stores:
        store.wait()


def write_out(volts, result, volts_out, sum_out, max_out, held_volts, held_result, load_sem, store_sem):
    pairs, rows = volts.shape[:2]
    part = rows // PIECES
    loads, stores = [], []
    for i in range(PIECES):
        at = pl.ds(i * part, part)
        moves = [(volts.at[p, at], held_volts.at[p, at], volts_out.at[p, at]) for p in range(pairs)]
        moves.append((result.at[0, at], held_result.at[0, at], sum_out.at[at]))
        moves.append((result.at[1, at], held_result.at[1, at], max_out.at[at]))
        for src, held, dst in moves:
            n = len(loads)
            loads.append(pltpu.make_async_copy(src, held, load_sem.at[n]))
            stores.append(pltpu.make_async_copy(held, dst, store_sem.at[n]))
    for load in loads:
        load.start()
    for load, store in zip(loads, stores):
        load.wait()
        store.start()
    for store in stores:
        store.wait()


def on_device(mesh_sizes, conductance, valid_mask, focal_cells, initial_volts):
    rows, columns = conductance.shape
    pairs = initial_volts.shape[0]
    tiles = columns // LANES
    n_pair, n_row, n_col = mesh_sizes
    sizes = (pairs, rows, tiles, n_pair, n_row, n_col)
    wide, tall, fold, quarter = tiles + 1, rows + 32, rows // 4, rows // 4
    n_dots = 2 * STEPS * pairs
    others = n_pair - 1
    arrays = min(2, pairs - NEAR_EARLY)
    pack_rows = 8 * ((quarter // 8 + 2 + 3) // 4)
    f32 = jnp.float32
    stay = pl.BlockSpec(memory_space=pltpu.HBM)
    raster = pltpu.VMEM((wide, tall, LANES), f32)
    volts, result = pl.pallas_call(
        functools.partial(kernel, sizes),
        out_shape=(
            jax.ShapeDtypeStruct((pairs, rows, columns), f32),
            jax.ShapeDtypeStruct((2, rows, columns), f32),
        ),
        in_specs=[stay, stay, pl.BlockSpec(memory_space=pltpu.SMEM), stay],
        out_specs=(stay, stay),
        scratch_shapes=[
            pltpu.VMEM((tiles, rows, LANES), f32),
            pltpu.VMEM((tiles, rows, LANES), jnp.int32),
            pltpu.VMEM((pairs, wide, tall, LANES), f32),
            raster,
            raster,
            raster,
            raster,
            raster,
            raster,
            raster,
            pltpu.VMEM((STEPS, pairs, wide, tall, LANES), f32),
            pltpu.VMEM((fold, LANES), f32),
            pltpu.VMEM((fold, LANES), f32),
            pltpu.VMEM((fold + 16, LANES), f32),
            pltpu.VMEM((fold + 16, LANES), f32),
            pltpu.VMEM((n_dots, 8, LANES), f32),
            pltpu.VMEM((n_dots, LANES), f32),
            pltpu.VMEM((n_col, n_dots, LANES), f32),
            pltpu.VMEM((n_row, n_dots, LANES), f32),
            pltpu.VMEM((2, rows, columns), f32),
            pltpu.VMEM((2, arrays, quarter, columns), f32),
            pltpu.VMEM((arrays, quarter, columns), f32),
            pltpu.VMEM((arrays, quarter, columns), f32),
            pltpu.VMEM((others, pairs, wide, quarter + 32, LANES), f32),
            pltpu.VMEM((others, STEPS, pairs, wide, quarter + 32, LANES), f32),
            pltpu.VMEM((others, pack_rows, LANES), f32),
            pltpu.VMEM((others, pack_rows, LANES), f32),
            pltpu.VMEM((8, LANES), jnp.int32),
            pltpu.VMEM((others, 8, LANES), jnp.int32),
            pltpu.VMEM((8 * ((STEPS * pairs + 7) // 8), LANES), f32),
            pltpu.VMEM((others, 8 * ((STEPS * pairs + 7) // 8), LANES), f32),
            pltpu.SemaphoreType.DMA(((2 + pairs) * tiles,)),
            pltpu.SemaphoreType.DMA((pairs * tiles + 7,)),
            pltpu.SemaphoreType.DMA((10,)),
            pltpu.SemaphoreType.DMA((10,)),
            pltpu.SemaphoreType.DMA((2, max(n_col, n_row) - 1)),
            pltpu.SemaphoreType.DMA((2, max(n_col, n_row) - 1)),
            pltpu.SemaphoreType.DMA((18,)),
            pltpu.SemaphoreType.DMA((18,)),
            pltpu.SemaphoreType.DMA((20,)),
            pltpu.SemaphoreType.DMA((20,)),
        ],
        compiler_params=pltpu.CompilerParams(
            collective_id=0, has_side_effects=True, vmem_limit_bytes=int(61 * 1024 * 1024)
        ),
    )(conductance, valid_mask, focal_cells, initial_volts)
    flat = jax.ShapeDtypeStruct((rows, columns), f32)
    return pl.pallas_call(
        write_out,
        out_shape=(jax.ShapeDtypeStruct((pairs, rows, columns), f32), flat, flat),
        in_specs=[stay, stay],
        out_specs=(stay, stay, stay),
        scratch_shapes=[
            pltpu.VMEM((pairs, rows, columns), f32),
            pltpu.VMEM((2, rows, columns), f32),
            pltpu.SemaphoreType.DMA((PIECES * (pairs + 2),)),
            pltpu.SemaphoreType.DMA((PIECES * (pairs + 2),)),
        ],
    )(volts, result)


def solution(mesh):
    in_specs = (P("row", "col"), P("row", "col"), P("pair", None), P("pair", "row", "col"))
    out_specs = (P("pair", "row", "col"), P("row", "col"), P("row", "col"))
    sizes = (mesh.shape["pair"], mesh.shape["row"], mesh.shape["col"])
    return jax.shard_map(
        functools.partial(on_device, sizes), mesh=mesh, in_specs=in_specs, out_specs=out_specs, check_vma=False
    )
```

```python
import functools

import jax
import jax.numpy as jnp
from jax import lax
from jax.experimental import pallas as pl
from jax.experimental.pallas import tpu as pltpu
from jax.sharding import PartitionSpec as P

MESH = pl.DeviceIdType.MESH
LEAKAGE = 0.01
STEPS = 6
LANES = 128
EDGE = 8
OWN = 16
BLOCK = 32
SWEEP = 64
HALF_BLOCK = 32
NEAR_EARLY = 1
PIECES = 2


def lane_ids(height):
    return lax.broadcasted_iota(jnp.int32, (height, LANES), 1)


def east(tiles):
    last = lane_ids(tiles[0].shape[0]) == LANES - 1
    rolled = [pltpu.roll(tile, LANES - 1, 1) for tile in tiles]
    return [jnp.where(last, rolled[(t + 1) % len(tiles)], rolled[t]) for t in range(len(tiles))]


def west(tiles):
    first = lane_ids(tiles[0].shape[0]) == 0
    rolled = [pltpu.roll(tile, 1, 1) for tile in tiles]
    return [jnp.where(first, rolled[t - 1], rolled[t]) for t in range(len(tiles))]


def link(a, b):
    return jnp.where(jnp.minimum(a, b) > 0.0, 0.5 * (a + b), 0.0)


def solve_coefficients(totals):
    same = [totals[2 * k] for k in range(STEPS)]
    after = [totals[2 * k + 1] for k in range(STEPS)]
    nu = [same[1], after[1]]
    for k in range(1, STEPS - 1):
        nu.append(2.0 * same[k + 1] - nu[0])
        nu.append(2.0 * after[k + 1] - nu[1])
    rho = [same[0], after[0], nu[0]]
    for k in range(1, STEPS - 2):
        rho.append(2.0 * nu[k] - rho[k])
    gram = [[None] * STEPS for _ in range(STEPS)]
    gram[0][0] = rho[0] - rho[1]
    for j in range(1, STEPS):
        gram[0][j] = rho[j] - nu[j - 1]
    for i in range(STEPS - 1):
        for j in range(i, STEPS - 1):
            before = abs(j - 1)
            gram[i + 1][j + 1] = 0.5 * (nu[i + j] + nu[abs(i - j)]) - 0.25 * (
                nu[i + j + 1] + nu[abs(i - j - 1)] + nu[i + before] + nu[abs(i - before)]
            )
    right = list(rho)
    least = [3e-7 * gram[j][j] for j in range(STEPS)]
    inverse, factors = [], {}
    for j in range(STEPS):
        pivot = gram[j][j]
        usable = pivot > least[j]
        inverse.append(jnp.where(usable, 1.0 / jnp.where(usable, pivot, 1.0), 0.0))
        for i in range(j + 1, STEPS):
            factors[i, j] = gram[j][i] * inverse[j]
        for i in range(j + 1, STEPS):
            for m in range(i, STEPS):
                gram[i][m] = gram[i][m] - factors[i, j] * gram[j][m]
            right[i] = right[i] - factors[i, j] * right[j]
    out = [right[j] * inverse[j] for j in range(STEPS)]
    for i in reversed(range(STEPS)):
        for j in range(i + 1, STEPS):
            out[i] = out[i] - factors[j, i] * out[j]
    return out


def kernel(
    sizes,
    cond_in,
    mask_in,
    focal,
    volts_in,
    volts_out,
    result_out,
    stage_cond,
    stage_mask,
    volts,
    cond,
    link_e,
    link_n,
    scale,
    coef_c,
    coef_e,
    coef_n,
    basis,
    pack_e,
    pack_w,
    land_w,
    land_e,
    dots,
    message,
    gather_col,
    gather_row,
    result,
    late,
    late_prev,
    late_next,
    far_volts,
    far_basis,
    far_pack,
    land_pack,
    cells,
    far_cells,
    shares,
    far_shares,
    load_sem,
    store_sem,
    halo_send,
    halo_recv,
    red_send,
    red_recv,
    far_send,
    far_recv,
    ring_send,
    ring_recv,
):
    pairs, rows, tiles, n_pair, n_row, n_col = sizes
    wide = tiles + 1
    chunks = rows // 8
    fold = rows // 4
    fold_chunks = fold // 8
    quarter = rows // 4
    unit = quarter // 4
    my_pair, my_row, my_col = lax.axis_index("pair"), lax.axis_index("row"), lax.axis_index("col")

    def around(index, step, count):
        return lax.rem(index + (step + count), count)

    loads = []
    for t in range(tiles):
        lanes = pl.ds(t * LANES, LANES)
        loads.append(pltpu.make_async_copy(cond_in.at[:, lanes], stage_cond.at[t], load_sem.at[len(loads)]))
        loads.append(pltpu.make_async_copy(mask_in.at[:, lanes], stage_mask.at[t], load_sem.at[len(loads)]))
        for p in range(pairs):
            loads.append(
                pltpu.make_async_copy(
                    volts_in.at[p, :, lanes], volts.at[p, t, pl.ds(OWN, rows)], load_sem.at[len(loads)]
                )
            )
    for load in loads:
        load.start()

    north, south = around(my_row, -1, n_row), around(my_row, 1, n_row)
    westward, eastward = around(my_col, -1, n_col), around(my_col, 1, n_col)
    partners = [{"col": around(my_col, step, n_col)} for step in range(1, n_col)]
    partners += [{"row": around(my_row, step, n_row)} for step in range(1, n_row)]
    partners += [{"row": r, "col": c} for r in (north, south) for c in (westward, eastward)]
    partners += [{"pair": around(my_pair, step, n_pair)} for step in range(1, n_pair)]
    barrier = pltpu.get_barrier_semaphore()
    for partner in partners:
        pl.semaphore_signal(barrier, inc=1, device_id=partner, device_id_type=MESH)

    zero = jnp.zeros((8, LANES), jnp.float32)
    for start in (0, rows + 3 * 8):
        at = pl.ds(start, 8)
        for t in range(wide):
            for ref in (cond, scale, link_n, coef_n):
                ref[t, at, :] = zero
            for p in range(pairs):
                volts[p, t, at, :] = zero
                for k in range(STEPS):
                    basis[k, p, t, at, :] = zero
    for start in (0, quarter + 3 * 8):
        at = pl.ds(start, 8)
        for s in range(n_pair - 1):
            for p in range(pairs):
                for t in range(wide):
                    far_volts[s, p, t, at, :] = zero
                    for k in range(STEPS):
                        far_basis[s, k, p, t, at, :] = zero
    row_of = lax.broadcasted_iota(jnp.int32, (8, LANES), 0)
    packed_cells = jnp.zeros((8, LANES), jnp.int32)
    for p in range(pairs):
        for j in range(2):
            packed_cells = jnp.where(row_of == 2 * p + j, focal[p, j], packed_cells)
    cells[...] = packed_cells

    for load in loads:
        load.wait()

    def own_cond(c, carry):
        at = pl.ds(pl.multiple_of(8 * c, 8), 8)
        to = pl.ds(pl.multiple_of(OWN + 8 * c, 8), 8)
        for t in range(tiles):
            cond[t, to, :] = stage_cond[t, at, :] * stage_mask[t, at, :].astype(jnp.float32)
        return carry

    lax.fori_loop(0, chunks, own_cond, 0)

    lane = lane_ids(8)

    def pack(c, carry):
        for side, tile, ref in ((0, 0, pack_w), (1, tiles - 1, pack_e)):
            packed = jnp.zeros((8, LANES), jnp.float32)
            for g in range(4):
                at = pl.ds(pl.multiple_of(OWN + g * fold + 8 * c, 8), 8)
                fields = [volts[p, tile, at, :] for p in range(pairs)] + [cond[tile, at, :]]
                for f, value in enumerate(fields):
                    low = 32 * g + 8 * f
                    first = 0 if side == 0 else LANES - 8
                    shift = (low - first) % LANES
                    moved = pltpu.roll(value, shift, 1) if shift else value
                    packed = jnp.where((lane >= low) & (lane < low + 8), moved, packed)
            ref[pl.ds(pl.multiple_of(8 * c, 8), 8), :] = packed
        return carry

    lax.fori_loop(0, fold_chunks, pack, 0)
    pl.semaphore_wait(barrier, len(partners))

    top, bottom = pl.ds(OWN, 8), pl.ds(OWN + rows - 8, 8)
    over, under = pl.ds(OWN - 8, 8), pl.ds(OWN + rows, 8)
    mid = pl.ds(8, fold)
    halo = [
        (volts.at[:, pl.ds(0, tiles), top], volts.at[:, pl.ds(0, tiles), under], {"row": north}),
        (cond.at[pl.ds(0, tiles), top], cond.at[pl.ds(0, tiles), under], {"row": north}),
        (volts.at[:, pl.ds(0, tiles), bottom], volts.at[:, pl.ds(0, tiles), over], {"row": south}),
        (cond.at[pl.ds(0, tiles), bottom], cond.at[pl.ds(0, tiles), over], {"row": south}),
        (pack_w, land_e.at[mid], {"col": westward}),
        (pack_e, land_w.at[mid], {"col": eastward}),
        (pack_w.at[pl.ds(0, 8)], land_e.at[pl.ds(fold + 8, 8)], {"row": north, "col": westward}),
        (pack_w.at[pl.ds(fold - 8, 8)], land_e.at[pl.ds(0, 8)], {"row": south, "col": westward}),
        (pack_e.at[pl.ds(0, 8)], land_w.at[pl.ds(fold + 8, 8)], {"row": north, "col": eastward}),
        (pack_e.at[pl.ds(fold - 8, 8)], land_w.at[pl.ds(0, 8)], {"row": south, "col": eastward}),
    ]
    halo = [
        pltpu.make_async_remote_copy(
            src_ref=src,
            dst_ref=dst,
            send_sem=halo_send.at[i],
            recv_sem=halo_recv.at[i],
            device_id=who,
            device_id_type=MESH,
        )
        for i, (src, dst, who) in enumerate(halo)
    ]
    for copy in halo:
        copy.start()

    ahead = (1, n_pair - 1, 2)
    owners = [around(my_pair, step, n_pair) for step in ahead]
    early = (min(NEAR_EARLY, pairs), min(NEAR_EARLY, pairs), pairs)
    moves = {}

    def give(s, kind, src, dst):
        slot = 5 * s + len([key for key in moves if key[0] == s])
        moves[s, kind] = pltpu.make_async_remote_copy(
            src_ref=src,
            dst_ref=dst,
            send_sem=far_send.at[slot],
            recv_sem=far_recv.at[slot],
            device_id={"pair": owners[s]},
            device_id_type=MESH,
        )
        moves[s, kind].start()

    def give_main(s):
        if not early[s]:
            return
        start = pl.multiple_of(OWN + owners[s] * quarter, 8)
        give(
            s,
            "main",
            volts.at[pl.ds(0, early[s]), pl.ds(0, tiles), pl.ds(start, quarter)],
            far_volts.at[s, pl.ds(0, early[s]), pl.ds(0, tiles), pl.ds(OWN, quarter)],
        )

    def give_border(s):
        if not early[s]:
            return
        start = OWN + owners[s] * quarter
        for kind, offset in (("over", -EDGE), ("under", quarter)):
            give(
                s,
                kind,
                volts.at[pl.ds(0, early[s]), pl.ds(0, tiles), pl.ds(pl.multiple_of(start + offset, 8), EDGE)],
                far_volts.at[s, pl.ds(0, early[s]), pl.ds(0, tiles), pl.ds(OWN + offset, EDGE)],
            )
        give(s, "pack", far_pack.at[s], land_pack.at[s])
        give(s, "cells", cells, far_cells.at[s])

    give_main(0)
    give_main(1)
    give_main(2)
    for copy in halo:
        copy.wait()

    has_n = (my_row > 0).astype(jnp.float32)
    has_s = (my_row < n_row - 1).astype(jnp.float32)
    has_w = (my_col > 0).astype(jnp.float32)
    has_e = (my_col < n_col - 1).astype(jnp.float32)
    for t in range(tiles):
        cond[t, over, :] = cond[t, over, :] * has_n
        cond[t, under, :] = cond[t, under, :] * has_s

    def unpack(source, g, to, keep):
        left = land_w[source, :]
        right = land_e[source, :]
        for f in range(pairs + 1):
            low = 32 * g + 8 * f
            a = pltpu.roll(left, (LANES - 8 - low) % LANES, 1)
            b = pltpu.roll(right, (LANES - low) % LANES, 1) if low else right
            if f == pairs:
                a, b = a * (has_w * keep), b * (has_e * keep)
            value = jnp.where(lane < 8, b, jnp.where(lane >= LANES - 8, a, 0.0))
            if f == pairs:
                cond[tiles, to, :] = value
            else:
                volts[f, tiles, to, :] = value

    def unpack_chunk(c, carry):
        for g in range(4):
            unpack(
                pl.ds(pl.multiple_of(8 + 8 * c, 8), 8),
                g,
                pl.ds(pl.multiple_of(OWN + g * fold + 8 * c, 8), 8),
                1.0,
            )
        return carry

    lax.fori_loop(0, fold_chunks, unpack_chunk, 0)
    unpack(pl.ds(0, 8), 3, over, has_n)
    unpack(pl.ds(fold + 8, 8), 0, under, has_s)

    far_rows = quarter + 2 * EDGE

    def pack_place(j, p):
        return 32 * (j % 4) + 16 * p

    for s in range(n_pair - 1):
        start = OWN - EDGE + owners[s] * quarter
        for c in range(far_pack.shape[1] // 8):
            packed = jnp.zeros((8, LANES), jnp.float32)
            for j in range(4 * c, min(4 * c + 4, far_rows // 8)):
                for p in range(early[s]):
                    low = pack_place(j, p)
                    value = volts[p, tiles, pl.ds(pl.multiple_of(start + 8 * j, 8), 8), :]
                    moved = pltpu.roll(value, (low + 8) % LANES, 1)
                    packed = jnp.where((lane >= low) & (lane < low + 16), moved, packed)
            far_pack[s, pl.ds(8 * c, 8), :] = packed
    give_border(0)
    give_border(1)
    give_border(2)

    def take(s):
        for kind in ("main", "over", "under", "pack", "cells"):
            moves[s, kind].wait_recv()
        for j in range(far_rows // 8):
            for p in range(early[s]):
                moved = pltpu.roll(
                    land_pack[s, pl.ds(8 * (j // 4), 8), :], (2 * LANES - 8 - pack_place(j, p)) % LANES, 1
                )
                far_volts[s, p, tiles, pl.ds(8 + 8 * j, 8), :] = jnp.where(
                    (lane < 8) | (lane >= LANES - 8), moved, 0.0
                )

    def sweep_own(body, carry=(), height=SWEEP):
        def step(c, carry):
            return body(pl.multiple_of(OWN + height * c, 8), height, carry)

        return lax.fori_loop(0, rows // height, step, carry)

    def sweep_border(body):
        def step(i, carry):
            return body(pl.multiple_of(OWN - 8 + i * (rows + 8), 8), 8, carry)

        lax.fori_loop(0, 2, step, ())

    def links_rows(start, height, carry):
        at = pl.ds(start, height)
        here = [cond[t, at, :] for t in range(wide)]
        right = [link(a, b) for a, b in zip(here, east(here))]
        left = west(right)
        for t in range(wide):
            up = link(here[t], cond[t, pl.ds(start - 1, height), :])
            down = link(here[t], cond[t, pl.ds(start + 1, height), :])
            diagonal = up + down + left[t] + right[t] + LEAKAGE * here[t] + jnp.where(here[t] > 0.0, 0.0, 1.0)
            most = jnp.maximum(diagonal, 1.0)
            root = lax.rsqrt(most)
            root = root * (1.5 - 0.5 * most * root * root)
            link_e[t, at, :] = right[t]
            link_n[t, at, :] = up
            scale[t, at, :] = root
            coef_c[t, at, :] = 2.0 * jnp.maximum(1.0 - diagonal, 0.0)
        return carry

    sweep_border(links_rows)
    sweep_own(links_rows)

    width_all = tiles * LANES * n_col

    def coefficient_rows(start, height, carry):
        at = pl.ds(start, height)
        root = [scale[t, at, :] for t in range(wide)]
        root_e = east(root)
        for t in range(wide):
            coef_e[t, at, :] = 2.0 * link_e[t, at, :] * root[t] * root_e[t]
            coef_n[t, at, :] = 2.0 * link_n[t, at, :] * root[t] * scale[t, pl.ds(start - 1, height), :]
        return carry

    def start_rows(count, field, out, ids, shift, start, height, carry):
        at, up_at, down_at = pl.ds(start, height), pl.ds(start - 1, height), pl.ds(start + 1, height)
        base = pl.multiple_of(start + shift, 8)
        own_at = pl.ds(base, height)
        column = lane_ids(height)
        sub = lax.broadcasted_iota(jnp.int32, (height, LANES), 0)
        first = my_col * (tiles * LANES)
        columns = [first + t * LANES + column for t in range(tiles)]
        columns.append(first + jnp.where(column < 64, tiles * LANES, -LANES) + column)
        right = [link_e[t, own_at, :] for t in range(wide)]
        flat = (my_row * rows + base - OWN + sub) * width_all
        own = []
        for t in range(wide):
            value = cond[t, own_at, :]
            own.append(LEAKAGE * value + jnp.where(value > 0.0, 0.0, 1.0))
        for p in range(count):
            here = [field[p, t, at, :] for t in range(wide)]
            there = east(here)
            flow = [right[t] * (here[t] - there[t]) for t in range(wide)]
            flow_w = west(flow)
            for t in range(wide):
                total = flow[t] - flow_w[t] + own[t] * here[t]
                total = total + link_n[t, own_at, :] * (here[t] - field[p, t, up_at, :])
                total = total + link_n[t, pl.ds(base + 1, height), :] * (here[t] - field[p, t, down_at, :])
                cell = flat + columns[t]
                inject = jnp.where(cell == ids[2 * p], 1.0, 0.0) - jnp.where(cell == ids[2 * p + 1], 1.0, 0.0)
                out[0, p, t, at, :] = scale[t, own_at, :] * (inject - total)
        return carry

    sweep_border(coefficient_rows)
    sweep_own(coefficient_rows)
    start_own = functools.partial(
        start_rows, pairs, volts, basis, [focal[p, j] for p in range(pairs) for j in range(2)], 0
    )
    sweep_border(start_own)
    sweep_own(start_own)

    def advance(fields, basis, shift, k, start, height, sums):
        at, up_at, down_at = pl.ds(start, height), pl.ds(start - 1, height), pl.ds(start + 1, height)
        base = pl.multiple_of(start + shift, 8)
        own_at = pl.ds(base, height)
        final = k == STEPS - 1
        count = tiles if final else wide
        right = [coef_e[t, own_at, :] for t in range(wide)]
        out = []
        for p in range(fields):
            here = [basis[k, p, t, at, :] for t in range(wide)]
            there = east(here)
            back = west([right[t] * here[t] for t in range(wide)])
            same = jnp.zeros((height, LANES), jnp.float32)
            step = jnp.zeros((height, LANES), jnp.float32)
            for t in range(count):
                value = coef_c[t, own_at, :] * here[t] + right[t] * there[t] + back[t]
                value = value + coef_n[t, own_at, :] * basis[k, p, t, up_at, :]
                value = value + coef_n[t, pl.ds(base + 1, height), :] * basis[k, p, t, down_at, :]
                value = 0.5 * value if k < 2 else value - basis[k - 1, p, t, at, :]
                if not final:
                    basis[k + 1, p, t, at, :] = value
                if sums and t < tiles:
                    same = same + here[t] * here[t]
                    step = step + here[t] * value
            if sums:
                out += [sums[2 * p] + same, sums[2 * p + 1] + step]
        return tuple(out) if sums else sums

    def fold_rows(value):
        total = value[:8]
        for i in range(1, SWEEP // 8):
            total = total + value[8 * i : 8 * i + 8]
        return total

    for k in range(STEPS):
        if k < STEPS - 1:
            sweep_border(functools.partial(advance, pairs, basis, 0, k))
        tall_zero = jnp.zeros((SWEEP, LANES), jnp.float32)
        sums = sweep_own(functools.partial(advance, pairs, basis, 0, k), (tall_zero,) * (2 * pairs), SWEEP)
        for p in range(pairs):
            dots[(2 * k) * pairs + p] = fold_rows(sums[2 * p])
            dots[(2 * k + 1) * pairs + p] = fold_rows(sums[2 * p + 1])

    shift = my_pair * quarter
    half = far_rows // 2

    def sweep_far(body):
        def step(c, carry):
            return body(pl.multiple_of(8 + half * c, 8), half, carry)

        lax.fori_loop(0, 2, step, ())

    def far_pairs(s):
        if not early[s]:
            return
        take(s)
        ids = [far_cells[s, pl.ds(r, 1), :] for r in range(2 * pairs)]
        sweep_far(functools.partial(start_rows, early[s], far_volts.at[s], far_basis.at[s], ids, shift))
        for k in range(STEPS - 1):
            sweep_far(functools.partial(advance, early[s], far_basis.at[s], shift, k))

    n_dots = 2 * STEPS * pairs
    part = jnp.sum(dots[...], axis=1)
    message[...] = jnp.broadcast_to(jnp.sum(part, axis=1, keepdims=True), (n_dots, LANES))

    def reduce_start(axis, me, count, gather, phase):
        copies = []
        for step in range(1, count):
            copies.append(
                pltpu.make_async_remote_copy(
                    src_ref=message,
                    dst_ref=gather.at[me],
                    send_sem=red_send.at[phase, step - 1],
                    recv_sem=red_recv.at[phase, step - 1],
                    device_id={axis: around(me, step, count)},
                    device_id_type=MESH,
                )
            )
        for copy in copies:
            copy.start()
        gather[me] = message[...]
        return copies

    def reduce_end(copies, count, gather):
        for copy in copies:
            copy.wait()
        total = gather[0]
        for i in range(1, count):
            total = total + gather[i]
        return total

    copies = reduce_start("col", my_col, n_col, gather_col, 0)
    message[...] = reduce_end(copies, n_col, gather_col)
    copies = reduce_start("row", my_row, n_row, gather_row, 1)
    far_pairs(0)
    totals = reduce_end(copies, n_row, gather_row)
    parts = solve_coefficients([totals[j * pairs : (j + 1) * pairs] for j in range(2 * STEPS)])
    for k in range(STEPS):
        shares[pl.ds(k * pairs, pairs), :] = parts[k]
    tell = []
    slots = [s for s in range(n_pair - 1) if early[s]]
    for s in slots:
        tell.append(
            pltpu.make_async_remote_copy(
                src_ref=shares,
                dst_ref=far_shares.at[s],
                send_sem=far_send.at[15 + s],
                recv_sem=far_recv.at[15 + s],
                device_id={"pair": owners[s]},
                device_id_type=MESH,
            )
        )
        tell[-1].start()

    def volts_rows(which, field, basis, shares, shift, start, height, carry):
        at = pl.ds(start, height)
        for p in which:
            for t in range(wide):
                change = shares[pl.ds(p, 1), :] * basis[0, p, t, at, :]
                for k in range(1, STEPS):
                    change = change + shares[pl.ds(k * pairs + p, 1), :] * basis[k, p, t, at, :]
                value = field[p, t, at, :] + scale[t, pl.ds(pl.multiple_of(start + shift, 8), height), :] * change
                field[p, t, at, :] = value
        return carry

    for copy in moves.values():
        copy.wait_send()
    sweep_border(functools.partial(volts_rows, range(early[0], pairs), volts, basis, shares, 0))
    sweep_own(functools.partial(volts_rows, range(early[0], pairs), volts, basis, shares, 0))
    stores = []
    for t in range(tiles):
        for p in range(pairs):
            stores.append(
                pltpu.make_async_copy(
                    volts.at[p, t, pl.ds(OWN, rows)],
                    volts_out.at[p, :, pl.ds(t * LANES, LANES)],
                    store_sem.at[len(stores)],
                )
            )


    def currents(row, height, fields, store):
        start = pl.multiple_of(OWN + row, 8)
        own_at = pl.ds(start, height)
        right = [link_e[t, own_at, :] for t in range(wide)]
        total, peak = [None] * tiles, [None] * tiles
        for field, first, p in fields:
            at, up_at, down_at = pl.ds(first, height), pl.ds(first - 1, height), pl.ds(first + 1, height)
            here = [field[p, t, at, :] for t in range(wide)]
            there = east(here)
            flow = [jnp.abs(right[t] * (here[t] - there[t])) for t in range(wide)]
            flow_w = west(flow)
            for t in range(tiles):
                value = flow[t] + flow_w[t]
                value = value + jnp.abs(link_n[t, own_at, :] * (here[t] - field[p, t, up_at, :]))
                value = value + jnp.abs(link_n[t, pl.ds(start + 1, height), :] * (here[t] - field[p, t, down_at, :]))
                value = 0.5 * value
                total[t] = value if total[t] is None else total[t] + value
                peak[t] = value if peak[t] is None else jnp.maximum(peak[t], value)
        for t in range(tiles):
            store(pl.ds(t * LANES, LANES), total[t], peak[t])

    q_next, q_prev, q_far = owners
    def span(index, u):
        return pl.ds(pl.multiple_of(index * quarter + u * unit, unit), unit)

    def ring(slot, src, dst, who):
        copy = pltpu.make_async_remote_copy(
            src_ref=src,
            dst_ref=dst,
            send_sem=ring_send.at[slot],
            recv_sem=ring_recv.at[slot],
            device_id={"pair": who},
            device_id_type=MESH,
        )
        copy.start()
        return copy

    sent = {}

    def spread(u, name):
        at = span(my_pair, u)
        if name == "up":
            sent["up", u] = ring(u, result.at[:, at], result.at[:, at], q_next)
        else:
            sent["down", u] = ring(4 + u, result.at[:, at], result.at[:, at], q_prev)

    arrays = late.shape[1]
    near_pairs = range(early[0], pairs)
    in_block = BLOCK // unit
    for i in range(quarter // BLOCK):
        for n, (owner, target) in enumerate(((q_next, late_prev), (q_prev, late_next))):
            row = pl.multiple_of(owner * quarter + BLOCK * i, BLOCK)
            at = pl.ds(BLOCK * i, BLOCK)

            def store(lanes, total, peak, n=n, at=at):
                late[n, 0, at, lanes] = total
                if arrays > 1:
                    late[n, 1, at, lanes] = peak

            currents(row, BLOCK, [(volts, pl.multiple_of(OWN + row, 8), p) for p in near_pairs], store)
            for u in range(i * in_block, (i + 1) * in_block):
                part = pl.ds(u * unit, unit)
                sent["late", n, u] = ring(12 + 2 * u + n, late.at[n, :, part], target.at[:, part], owner)
    sweep_border(functools.partial(volts_rows, range(early[0]), volts, basis, shares, 0))
    sweep_own(functools.partial(volts_rows, range(early[0]), volts, basis, shares, 0))
    for store in stores:
        store.start()

    far_pairs(1)
    far_pairs(2)
    for s, told in zip(slots, tell):
        told.wait_recv()
        sweep_far(functools.partial(volts_rows, range(early[s]), far_volts.at[s], far_basis.at[s], far_shares.at[s], shift))
    for i in range(quarter // BLOCK):

        def own_block(h, carry, i=i):
            at = BLOCK * i + HALF_BLOCK * h
            row = pl.multiple_of(my_pair * quarter + at, HALF_BLOCK)
            fields = [(volts, pl.multiple_of(OWN + row, 8), p) for p in range(pairs)]
            for s in range(n_pair - 1):
                fields += [(far_volts.at[s], pl.multiple_of(OWN + at, 8), p) for p in range(early[s])]

            def store(lanes, total, peak):
                result[0, pl.ds(row, HALF_BLOCK), lanes] = total
                result[1, pl.ds(row, HALF_BLOCK), lanes] = peak

            currents(row, HALF_BLOCK, fields, store)
            return carry

        lax.fori_loop(0, BLOCK // HALF_BLOCK, own_block, 0)
        for u in range(i * in_block, (i + 1) * in_block):
            at, rows_of = span(my_pair, u), pl.ds(u * unit, unit)
            sent["late", 0, u].wait_recv()
            sent["late", 1, u].wait_recv()
            result[0, at, :] = result[0, at, :] + late_prev[0, rows_of, :] + late_next[0, rows_of, :]
            result[1, at, :] = jnp.maximum(
                result[1, at, :], jnp.maximum(late_prev[arrays - 1, rows_of, :], late_next[arrays - 1, rows_of, :])
            )
            spread(u, "up")
            spread(u, "down")

    def keep(index, slot, first, count):
        at = pl.ds(pl.multiple_of(index * quarter + first * unit, unit), count * unit)
        stores.append(pltpu.make_async_copy(result.at[:, at], result_out.at[:, at], store_sem.at[pairs * tiles + slot]))
        stores[-1].start()

    for i in range(2):
        sent["up", i].wait_recv()
        at = span(q_prev, i)
        sent["over", i] = ring(8 + i, result.at[:, at], result.at[:, at], q_next)
        sent["down", 2 + i].wait_recv()
        at = span(q_next, 2 + i)
        sent["over", 2 + i] = ring(10 + i, result.at[:, at], result.at[:, at], q_prev)
    keep(my_pair, 0, 0, 4)
    for i in range(2):
        sent["up", 2 + i].wait_recv()
        sent["down", i].wait_recv()
    keep(q_prev, 1, 0, 4)
    keep(q_next, 2, 0, 4)
    for i in range(2):
        sent["over", i].wait_recv()
        sent["over", 2 + i].wait_recv()
        keep(q_far, 3 + 2 * i, i, 1)
        keep(q_far, 4 + 2 * i, 2 + i, 1)
    for copy in sent.values():
        copy.wait_send()
    for copy in tell:
        copy.wait_send()
    for store in stores:
        store.wait()


def write_out(volts, result, volts_out, sum_out, max_out, held_volts, held_result, load_sem, store_sem):
    pairs, rows = volts.shape[:2]
    part = rows // PIECES
    loads, stores = [], []
    for i in range(PIECES):
        at = pl.ds(i * part, part)
        moves = [(volts.at[p, at], held_volts.at[p, at], volts_out.at[p, at]) for p in range(pairs)]
        moves.append((result.at[0, at], held_result.at[0, at], sum_out.at[at]))
        moves.append((result.at[1, at], held_result.at[1, at], max_out.at[at]))
        for src, held, dst in moves:
            n = len(loads)
            loads.append(pltpu.make_async_copy(src, held, load_sem.at[n]))
            stores.append(pltpu.make_async_copy(held, dst, store_sem.at[n]))
    for load in loads:
        load.start()
    for load, store in zip(loads, stores):
        load.wait()
        store.start()
    for store in stores:
        store.wait()


def on_device(mesh_sizes, conductance, valid_mask, focal_cells, initial_volts):
    rows, columns = conductance.shape
    pairs = initial_volts.shape[0]
    tiles = columns // LANES
    n_pair, n_row, n_col = mesh_sizes
    sizes = (pairs, rows, tiles, n_pair, n_row, n_col)
    wide, tall, fold, quarter = tiles + 1, rows + 32, rows // 4, rows // 4
    n_dots = 2 * STEPS * pairs
    others = n_pair - 1
    arrays = min(2, pairs - NEAR_EARLY)
    pack_rows = 8 * ((quarter // 8 + 2 + 3) // 4)
    f32 = jnp.float32
    stay = pl.BlockSpec(memory_space=pltpu.HBM)
    raster = pltpu.VMEM((wide, tall, LANES), f32)
    volts, result = pl.pallas_call(
        functools.partial(kernel, sizes),
        out_shape=(
            jax.ShapeDtypeStruct((pairs, rows, columns), f32),
            jax.ShapeDtypeStruct((2, rows, columns), f32),
        ),
        in_specs=[stay, stay, pl.BlockSpec(memory_space=pltpu.SMEM), stay],
        out_specs=(stay, stay),
        scratch_shapes=[
            pltpu.VMEM((tiles, rows, LANES), f32),
            pltpu.VMEM((tiles, rows, LANES), jnp.int32),
            pltpu.VMEM((pairs, wide, tall, LANES), f32),
            raster,
            raster,
            raster,
            raster,
            raster,
            raster,
            raster,
            pltpu.VMEM((STEPS, pairs, wide, tall, LANES), f32),
            pltpu.VMEM((fold, LANES), f32),
            pltpu.VMEM((fold, LANES), f32),
            pltpu.VMEM((fold + 16, LANES), f32),
            pltpu.VMEM((fold + 16, LANES), f32),
            pltpu.VMEM((n_dots, 8, LANES), f32),
            pltpu.VMEM((n_dots, LANES), f32),
            pltpu.VMEM((n_col, n_dots, LANES), f32),
            pltpu.VMEM((n_row, n_dots, LANES), f32),
            pltpu.VMEM((2, rows, columns), f32),
            pltpu.VMEM((2, arrays, quarter, columns), f32),
            pltpu.VMEM((arrays, quarter, columns), f32),
            pltpu.VMEM((arrays, quarter, columns), f32),
            pltpu.VMEM((others, pairs, wide, quarter + 32, LANES), f32),
            pltpu.VMEM((others, STEPS, pairs, wide, quarter + 32, LANES), f32),
            pltpu.VMEM((others, pack_rows, LANES), f32),
            pltpu.VMEM((others, pack_rows, LANES), f32),
            pltpu.VMEM((8, LANES), jnp.int32),
            pltpu.VMEM((others, 8, LANES), jnp.int32),
            pltpu.VMEM((8 * ((STEPS * pairs + 7) // 8), LANES), f32),
            pltpu.VMEM((others, 8 * ((STEPS * pairs + 7) // 8), LANES), f32),
            pltpu.SemaphoreType.DMA(((2 + pairs) * tiles,)),
            pltpu.SemaphoreType.DMA((pairs * tiles + 7,)),
            pltpu.SemaphoreType.DMA((10,)),
            pltpu.SemaphoreType.DMA((10,)),
            pltpu.SemaphoreType.DMA((2, max(n_col, n_row) - 1)),
            pltpu.SemaphoreType.DMA((2, max(n_col, n_row) - 1)),
            pltpu.SemaphoreType.DMA((18,)),
            pltpu.SemaphoreType.DMA((18,)),
            pltpu.SemaphoreType.DMA((20,)),
            pltpu.SemaphoreType.DMA((20,)),
        ],
        compiler_params=pltpu.CompilerParams(
            collective_id=0, has_side_effects=True, vmem_limit_bytes=int(61 * 1024 * 1024)
        ),
    )(conductance, valid_mask, focal_cells, initial_volts)
    flat = jax.ShapeDtypeStruct((rows, columns), f32)
    return pl.pallas_call(
        write_out,
        out_shape=(jax.ShapeDtypeStruct((pairs, rows, columns), f32), flat, flat),
        in_specs=[stay, stay],
        out_specs=(stay, stay, stay),
        scratch_shapes=[
            pltpu.VMEM((pairs, rows, columns), f32),
            pltpu.VMEM((2, rows, columns), f32),
            pltpu.SemaphoreType.DMA((PIECES * (pairs + 2),)),
            pltpu.SemaphoreType.DMA((PIECES * (pairs + 2),)),
        ],
    )(volts, result)


def solution(mesh):
    in_specs = (P("row", "col"), P("row", "col"), P("pair", None), P("pair", "row", "col"))
    out_specs = (P("pair", "row", "col"), P("row", "col"), P("row", "col"))
    sizes = (mesh.shape["pair"], mesh.shape["row"], mesh.shape["col"])
    return jax.shard_map(
        functools.partial(on_device, sizes), mesh=mesh, in_specs=in_specs, out_specs=out_specs, check_vma=False
    )
```
